768 devices in a mesh: tile: 24 (over z, core), lev: 32 (over y, x).
Axes of the slice: x: 4, y: 8, z: 12, core: 2. Of those that a mesh axis runs over, the one named last changes fastest.
Arguments:
- adj_arrival: float32 [128, 4, 192, 512], P('lev', None, 'tile'), may hold values from -6 to 6
- vert_coef: float32 [3, 128, 192, 512], P(None, 'lev', 'tile'), may hold values from 0.1 to 0.9
- stencil_weight: bfloat16 [192, 4, 16, 512], P('tile'), may hold values from -1.5 to 1.5
- stencil_cols: int32 [192, 4, 16, 512], P('tile'), may hold values from 0 to 511, as said below
- dep_owner: int32 [192, 4], P('tile'), may hold values from 0 to 23, all different within a row; in each aligned block of 8 rows (0 to 7, 8 to 15, ...) at most 2 rows name the same one
- dep_slot: int32 [192, 4], P('tile'), may hold values from 0 to 7
Outputs:
- adj_departure: float32 [128, 4, 192, 512], P('lev', None, 'tile')
The draws below stay inside these ranges and needn't reach their ends.
Inputs may be any that keep to these rules, and one draw needn't show every extreme that they name: `dep_owner`: each row holds 4 different owners. Among the rows of one tile (aligned blocks of 8 rows) no owner is named more than 2 times, a bound that some block reaches. `stencil_cols`: the 16 source columns of a departure point form a 4 by 4 patch of columns, rows of 16 columns apart, taken cyclically within the block.
All inputs are finite; a program needn't handle non-finite values.
Results may differ from the reference program's by a relative error of at most 0.0029.
Values sent between devices are 32-bit elements; how exact they have to be, the bound alone decides.
No kernel may reach another device: no remote copies, remote signals or barrier semaphores. Data moves between devices by JAX's collectives and lax.ppermute only.
A program may use at most 32 MiB of HBM per device.

```python
import math
import jax
import jax.numpy as jnp
import numpy as np
from jax import lax

FLD = 4
STEN = 16
COLS = 512
BLK_DEV = 8
DEPS = 4
NB = 192
LEV = 128
CAP = 2
N_TILE = 24


def draw_stencil_cols(key, part):
    key = jax.random.fold_in(key, 7)
    base = jax.random.randint(key, (NB, DEPS, 1, COLS), 0, COLS, dtype=jnp.int32)
    first = jnp.arange(COLS, dtype=jnp.int32)[None, None, None, :] == 0
    base = jnp.where(first, COLS - 1, base)
    points = jnp.arange(STEN, dtype=jnp.int32)
    offsets = (points % 4 + 16 * (points // 4)).reshape(1, 1, STEN, 1)
    return ((base + offsets) % COLS).astype(jnp.int32)


def place_ends(array, key, low, top_value):
    shape = array.shape
    place = [jax.random.randint(jax.random.fold_in(key, axis), (), 0, shape[axis]) for axis in range(len(shape))]
    array = array.at[tuple(place)].set(low)
    longest = shape.index(max(shape))
    place[longest] = (place[longest] + 1) % shape[longest]
    return array.at[tuple(place)].set(top_value)


def shard_levels(own_key, extent, cuts, smallest, largest):
    level, own = 1.0, jax.random.fold_in(own_key, 6)
    for axis_at, parts in cuts:
        steps = jnp.exp(jax.random.uniform(jax.random.fold_in(own, axis_at), (parts,), jnp.float32, smallest / len(cuts), largest / len(cuts)))
        level = level * jnp.repeat(steps, extent[axis_at] // parts).reshape([-1 if axis == axis_at else 1 for axis in range(len(extent))])
    return level


def assign_block(key, own, number, rows, amount, top, reach, lean):
    ranking = jax.random.permutation(key, amount)
    heavy_load, common = portions_of(amount, rows * top, reach, lean, True), portions_of(amount, rows * top, reach, lean, False)
    places = jnp.arange(amount)

    def named(lengths, rotation):
        used = int((lengths > 0).sum())
        fixed = max(1, used // 4)
        passed = fixed + (places - fixed + rotation * (used - fixed)) % max(1, amount - fixed)
        return jnp.zeros((amount,), jnp.int32).at[ranking[jnp.where(places < fixed, places, passed)]].set(jnp.asarray(lengths, jnp.int32))

    lengths = jnp.where(number % 4 == 0, named(heavy_load, number // 4), named(common, number - number // 4 - 1))
    mixed = jax.random.permutation(jax.random.fold_in(own, 3), amount)
    giver, receiver = mixed[0:amount // 2 * 2:2], mixed[1:amount // 2 * 2:2]
    margin = jnp.minimum(lengths[giver] - 1, reach - lengths[receiver]) // 2
    margin = jnp.where((giver == ranking[0]) | (receiver == ranking[0]) | (lengths[receiver] == 0), 0, jnp.maximum(margin, 0))
    passed = jax.random.randint(jax.random.fold_in(own, 4), (amount // 2,), 0, 1 << 20) % (margin + 1)
    lengths = lengths.at[giver].add(-passed).at[receiver].add(passed)
    items = jnp.searchsorted(jnp.cumsum(lengths), jnp.arange(rows * top), side="right").astype(jnp.int32)
    table = items.reshape(top, rows).T
    table = table[jax.random.permutation(jax.random.fold_in(own, 1), rows)]
    rotation = jax.random.randint(jax.random.fold_in(own, 2), (rows, 1), 0, top)
    return jnp.take_along_axis(table, (jnp.arange(top)[None, :] + rotation) % top, axis=1)


def portions_of(count, total, reach, lean, full):
    portions = [(1 << 20) // math.isqrt(standing ** lean) + 1 for standing in range(1, count + 1)]
    largest = reach if full else min(reach, max(-(-total // count), total * portions[0] // sum(portions)))
    least = 1 if total - largest >= count - 1 else 0
    holding, surplus = [largest] + [least] * (count - 1), total - largest - least * (count - 1)
    while surplus > 0:
        movable = [i for i in range(1, count) if holding[i] < largest] or [i for i in range(1, count) if holding[i] < reach]
        pool, budget = sum([portions[i] for i in movable]), surplus
        for i in movable:
            extra = min(reach - holding[i], max(1, budget * portions[i] // pool), surplus)
            holding[i] = holding[i] + extra
            surplus = surplus - extra
    return np.array(holding)


def noise(own_key, extent, width, limit, pieces=(), held_as=jnp.bfloat16):
    values = jax.random.normal(own_key, extent, jnp.float32) * width
    if len(pieces) > 0:
        values = shard_levels(own_key, extent, pieces, -0.22, 0.18) * values
    return jnp.clip(values, min=-limit, max=limit).astype(held_as)


def setup_inputs(seed: int = 0) -> dict:
    key_of = jax.random.split(jax.random.key(seed), 7)
    adj_arrival = noise(key_of[0], (LEV, FLD, NB, COLS), 1.0, 6.0, ((0, 32), (2, 24)), jnp.float32)
    vert_coef = jnp.clip(0.1 + 0.79999997 * jax.random.uniform(key_of[1], (3, LEV, NB, COLS), jnp.float32) ** shard_levels(key_of[1], (3, LEV, NB, COLS), ((1, 32), (2, 24)), -0.2, 0.2), 0.1, 0.9)
    stencil_weight = noise(key_of[2], (NB, DEPS, STEN, COLS), STEN ** -0.5, 1.5, ((0, 24),))
    stencil_cols = draw_stencil_cols(jax.random.fold_in(key_of[6], 71), 0)
    dep_owner_keys = jax.random.split(jax.random.fold_in(key_of[4], 1), NB // BLK_DEV)
    dep_owner_turns = jax.random.permutation(jax.random.fold_in(key_of[4], 3), NB // BLK_DEV)
    dep_owner = jax.vmap(lambda own, number: assign_block(jax.random.fold_in(key_of[4], 2), own, number, BLK_DEV, N_TILE, DEPS, CAP, 2))(dep_owner_keys, dep_owner_turns).reshape((NB, DEPS))
    dep_slot = place_ends(jax.random.randint(key_of[5], (NB, DEPS), 0, BLK_DEV), jax.random.fold_in(key_of[5], 1), 0, BLK_DEV - 1).astype(jnp.int32)
    return dict(adj_arrival=adj_arrival, vert_coef=vert_coef, stencil_weight=stencil_weight, stencil_cols=stencil_cols, dep_owner=dep_owner, dep_slot=dep_slot)


def reference(adj_arrival, vert_coef, stencil_weight, stencil_cols, dep_owner, dep_slot):
    below = vert_coef[0][:, None]
    middle = vert_coef[1][:, None]
    above = vert_coef[2][:, None]
    z_low = below * adj_arrival
    z_high = above * adj_arrival
    zero_level = jnp.zeros_like(adj_arrival[:1])
    vert_adj = jnp.concatenate([z_low[1:], zero_level], 0) + middle * adj_arrival + jnp.concatenate([zero_level, z_high[:-1]], 0)
    vert_low = vert_adj.astype(jnp.bfloat16)
    target = (dep_owner * BLK_DEV + dep_slot).astype(jnp.int32)
    blocks = jnp.transpose(vert_low, (2, 3, 0, 1))
    dep_ids = jnp.arange(DEPS, dtype=jnp.int32)[:, None, None]

    def step(carry, packed):
        block_in, weights, columns, where = packed
        values = weights.astype(jnp.float32)[:, :, :, None, None] * block_in.astype(jnp.float32)[None, None]
        contrib = jnp.zeros((DEPS, COLS, LEV, FLD), jnp.float32).at[dep_ids, columns].add(values)
        return carry.at[where].add(jnp.transpose(contrib, (0, 2, 3, 1))), None

    start = jnp.zeros((NB, LEV, FLD, COLS), jnp.float32)
    total, _ = lax.scan(step, start, (blocks, stencil_weight, stencil_cols, target))
    return jnp.transpose(total, (1, 2, 0, 3))
```

```python
import functools

import jax
import jax.numpy as jnp
from jax import lax
from jax.experimental import pallas as pl
from jax.experimental.pallas import tpu as pltpu
from jax.sharding import PartitionSpec as P

WIN = 32
SPAN = 96
LANES = 128
CAP = 2


def contrib_item(v_ref, w_ref, cols_ref, x_sc, w_sc, v_sc, p_sc):
    points, cols = cols_ref.shape[-2:]
    rows = v_ref.shape[-2]
    wins = cols // WIN
    d = cols_ref[0]
    rel = ((d - d[0:1] + cols // 2) & (cols - 1)) - cols // 2
    low = jnp.min(rel, axis=0, keepdims=True)
    base = (d[0:1] + low) & (cols - 1)
    x_sc[...] = rel - low + (base & (WIN - 1))
    w_sc[...] = w_ref[0].astype(jnp.float32)
    q = base // WIN
    v = v_ref[0].astype(jnp.float32)
    for i in range(wins):
        v_sc[i * rows:(i + 1) * rows, :] = jnp.where(q == i, v, 0.0).astype(jnp.bfloat16)
    place = lax.broadcasted_iota(jnp.int32, (SPAN, LANES), 0)
    for t in range(cols // LANES):
        part = slice(t * LANES, (t + 1) * LANES)
        acc = jnp.zeros((SPAN, LANES), jnp.float32)
        for s in range(points):
            acc = jnp.where(place == x_sc[s:s + 1, part], w_sc[s:s + 1, part], acc)
        p_sc[0:SPAN, part] = acc.astype(jnp.bfloat16)
    u = lax.dot_general(
        v_sc[...], p_sc[...], (((1,), (1,)), ((), ())), preferred_element_type=jnp.float32
    )
    lane = lax.broadcasted_iota(jnp.int32, (rows, LANES), 1)
    kept, passed = [], []
    for t in range(cols // LANES):
        u0, u1, u2, u3 = (u[(4 * t + j) * rows:(4 * t + j + 1) * rows] for j in range(4))
        kept.append(u0 + pltpu.roll(u1, WIN, 1))
        passed.append(pltpu.roll(u2, 2 * WIN, 1) + pltpu.roll(u3, 3 * WIN, 1))
    return [
        kept[t] + jnp.where(lane >= LANES // 2, passed[t], passed[t - 1]) for t in range(len(kept))
    ]


def contrib_kernel(groups, table, v_ref, w_ref, cols_ref, *rest):
    outs, (x_sc, w_sc, v_sc, p_sc) = rest[:groups], rest[groups:]
    rows, cols = v_ref.shape[-2:]
    step = pl.program_id(0)
    per = table.shape[1] // groups

    @pl.when(step == 0)
    def _():
        p_sc[SPAN:, :] = jnp.zeros((LANES - SPAN, cols), jnp.bfloat16)

    for g in range(groups):
        out = outs[g]

        @pl.when(step == g * per)
        def _():
            out[...] = jnp.zeros_like(out)
            ids = lax.broadcasted_iota(jnp.int32, (8, cols), 0)
            slots = jnp.zeros((8, cols), jnp.int32)
            for n in range(per):
                slots = jnp.where(ids == n, table[1, g * per + n], slots)
            out[per * rows:, :] = slots.astype(jnp.float32)

    @pl.when(table[0, step] >= 0)
    def _():
        parts = contrib_item(v_ref, w_ref, cols_ref, x_sc, w_sc, v_sc, p_sc)
        for g in range(groups):
            @pl.when(step // per == g)
            def _():
                at = pl.multiple_of((step - g * per) * rows, rows)
                for t, part in enumerate(parts):
                    outs[g][pl.ds(at, rows), t * LANES:(t + 1) * LANES] = part


def contributions(table, groups, deps, v, w, cols):
    steps = table.shape[1]
    per = steps // groups
    rows, width = v.shape[1:]
    points = w.shape[1]
    item = lambda i, table: (jnp.maximum(table[0, i], 0), 0, 0)
    block = lambda i, table: (jnp.maximum(table[0, i], 0) // deps, 0, 0)
    shape = (per * rows + 8, width)
    return pl.pallas_call(
        functools.partial(contrib_kernel, groups),
        grid_spec=pltpu.PrefetchScalarGridSpec(
            num_scalar_prefetch=1,
            grid=(steps,),
            in_specs=[
                pl.BlockSpec((1, rows, width), block),
                pl.BlockSpec((1, points, width), item),
                pl.BlockSpec((1, points, width), item),
            ],
            out_specs=[pl.BlockSpec(shape, lambda i, table: (0, 0))] * groups,
            scratch_shapes=[
                pltpu.VMEM((points, width), jnp.int32),
                pltpu.VMEM((points, width), jnp.float32),
                pltpu.VMEM((width // WIN * rows, width), jnp.bfloat16),
                pltpu.VMEM((LANES, width), jnp.bfloat16),
            ],
        ),
        out_shape=[jax.ShapeDtypeStruct(shape, jnp.float32)] * groups,
        compiler_params=pltpu.CompilerParams(dimension_semantics=("arbitrary",)),
        cost_estimate=pl.CostEstimate(
            flops=steps * 1200000000, bytes_accessed=steps * 100000, transcendentals=0
        ),
        name="contributions",
    )(table, v, w, cols)


def add_items(total, items, half, rows):
    per = items.shape[0] // rows
    for n in range(half * CAP, half * CAP + CAP):
        slot = items[per * rows + n:per * rows + n + 1, :]
        value = items[n * rows:(n + 1) * rows, :]
        total = [t + jnp.where(slot == float(b), value, 0.0) for b, t in enumerate(total)]
    return total


def merge_kernel(half, dense, blk, rows, *refs):
    out = refs[-1]
    width = out.shape[1]
    for c in range(0, width, LANES):
        part = pl.ds(c, LANES)
        if dense:
            total = [refs[0][b * rows:(b + 1) * rows, part] for b in range(blk)]
            sparse = refs[1:-1]
        else:
            total = [jnp.zeros((rows, LANES), jnp.float32)] * blk
            sparse = refs[:-1]
        for items in sparse:
            total = add_items(total, items.at[:, part], half, rows)
        for b in range(blk):
            out[b * rows:(b + 1) * rows, part] = total[b]


def merge(half, blk, rows, total, sparse):
    width = sparse[0].shape[1]
    args = ([] if total is None else [total]) + list(sparse)
    return pl.pallas_call(
        functools.partial(merge_kernel, half, total is not None, blk, rows),
        out_shape=jax.ShapeDtypeStruct((blk * rows, width), jnp.float32),
        cost_estimate=pl.CostEstimate(flops=1000000, bytes_accessed=1000000, transcendentals=0),
        name="merge",
    )(*args)


def finish_kernel(blk, rows, total_ref, other_ref, items_ref, out):
    width = out.shape[-1]
    for c in range(0, width, LANES):
        part = pl.ds(c, LANES)
        total = [
            total_ref[b * rows:(b + 1) * rows, part] + other_ref[b * rows:(b + 1) * rows, part]
            for b in range(blk)
        ]
        total = add_items(total, items_ref.at[:, part], 1, rows)
        out[:, :, part] = jnp.swapaxes(jnp.stack(total, 0), 0, 1)


def finish(blk, rows, total, other, items):
    return pl.pallas_call(
        functools.partial(finish_kernel, blk, rows),
        out_shape=jax.ShapeDtypeStruct((rows, blk, total.shape[1]), jnp.float32),
        name="finish",
    )(total, other, items)


def shards(adj_arrival, vert_coef, stencil_weight, stencil_cols, dep_owner, dep_slot):
    lev_dev, fields, blk, cols = adj_arrival.shape
    tiles, levels = lax.axis_size("tile"), lax.axis_size("lev")
    deps, points = stencil_weight.shape[1:3]
    items, rows = blk * deps, lev_dev * fields
    chips = tiles // 2
    far = chips // 2

    first = vert_coef[0, :1, None] * adj_arrival[:1]
    last = vert_coef[2, -1:, None] * adj_arrival[-1:]
    after = lax.ppermute(first, "lev", [(i + 1, i) for i in range(levels - 1)])
    before = lax.ppermute(last, "lev", [(i, i + 1) for i in range(levels - 1)])

    tile = lax.axis_index("tile")
    chip, core = tile // 2, tile % 2
    ahead = 1 - 2 * core
    owner, slot = dep_owner.reshape(items), dep_slot.reshape(items)
    number = jnp.arange(items, dtype=jnp.int32)
    rank = jnp.sum((owner[None, :] == owner[:, None]) & (number[None, :] < number[:, None]), axis=1)

    def group(distance, first_core):
        at = jnp.mod(chip + ahead * distance, chips) * 2
        return [(at + first_core, 0), (at + first_core, 1), (at + 1 - first_core, 0), (at + 1 - first_core, 1)]

    stages = [group(far, 1 - core)]
    for h in range(far - 1, 0, -1):
        stages.append(group(h, 1 - core) + group(-h, core))
    stages.append(group(0, 1 - core))
    wanted = [pair for stage in stages for pair in stage]
    want = jnp.stack([w for w, _ in wanted])
    turn = jnp.asarray([t for _, t in wanted], jnp.int32)
    match = (owner[None, :] == want[:, None]) & (rank[None, :] == turn[:, None])
    index = jnp.sum(jnp.where(match, number[None, :] + 1, 0), axis=1) - 1
    place = jnp.sum(jnp.where(match, slot[None, :], 0), axis=1)
    table = jnp.stack([index, place]).astype(jnp.int32)

    z_low = vert_coef[0, 1:, None] * adj_arrival[1:]
    z_high = vert_coef[2, :-1, None] * adj_arrival[:-1]
    vert_adj = (
        jnp.concatenate([z_low, after], 0)
        + vert_coef[1][:, None] * adj_arrival
        + jnp.concatenate([before, z_high], 0)
    )
    vert_low = vert_adj.astype(jnp.bfloat16).reshape(rows, blk, cols)
    v = jnp.transpose(vert_low, (1, 0, 2))
    w = stencil_weight.reshape(items, points, cols)
    places = stencil_cols.reshape(items, points, cols)

    sibling = [(t, t ^ 1) for t in range(tiles)]
    ring = [(t, (t + 2 * (1 - 2 * (t % 2))) % tiles) for t in range(tiles)]
    made, at = [], 0
    for stage in stages:
        size = len(stage)
        made.append(contributions(table[:, at:at + size], size // 4, deps, v, w, places))
        at += size

    arrived = lax.ppermute(made[0][0], "tile", ring)
    sums = [None, None]
    for h in range(far - 1, 0, -1):
        own, others = made[far - h]
        given = lax.ppermute(others, "tile", sibling)
        for half in range(2):
            sparse = [own, given] + ([arrived] if h == far - 1 else [])
            total = merge(half, blk, rows, sums[half], sparse)
            sums[half] = lax.ppermute(total, "tile", ring)
    here = made[far][0]
    swapped = lax.ppermute(merge(0, blk, rows, sums[0], [here]), "tile", sibling)
    result = finish(blk, rows, sums[1], swapped, here)
    return result.reshape(lev_dev, fields, blk, cols)


def solution(mesh):
    in_specs = (
        P("lev", None, "tile", None),
        P(None, "lev", "tile", None),
        P("tile", None, None, None),
        P("tile", None, None, None),
        P("tile", None),
        P("tile", None),
    )
    out_specs = P("lev", None, "tile", None)
    return jax.shard_map(shards, mesh=mesh, in_specs=in_specs, out_specs=out_specs, check_vma=False)
```

```python
import functools

import jax
import jax.numpy as jnp
from jax import lax
from jax.experimental import pallas as pl
from jax.experimental.pallas import tpu as pltpu
from jax.sharding import PartitionSpec as P

WIN = 32
SPAN = 96
LANES = 128
CAP = 2
MIB = 1024 * 1024


def stage_sizes(far):
    return [2 * CAP] + [4 * CAP] * (far - 1) + [2 * CAP]


def fill_table(chips, owner_ref, slot_ref, table, count):
    blk, deps = owner_ref.shape
    far = chips // 2
    tile = lax.axis_index("tile")
    chip, core = lax.div(tile, 2), lax.rem(tile, 2)
    ahead = 1 - 2 * core
    entries = sum(stage_sizes(far))

    def clear(n, _):
        table[0, n] = jnp.int32(-1)
        table[1, n] = jnp.int32(0)
        return 0

    lax.fori_loop(0, entries, clear, 0)

    def reset(n, _):
        count[n] = jnp.int32(0)
        return 0

    lax.fori_loop(0, 2 * chips, reset, 0)

    def enter(n, _):
        row, k = lax.div(n, deps), lax.rem(n, deps)
        owner = owner_ref[row, k]
        turn = count[owner]
        count[owner] = turn + 1
        away = lax.rem(ahead * (lax.div(owner, 2) - chip) + chips, chips)
        back = away > far
        distance = jnp.where(back, chips - away, away)
        own = (lax.rem(owner, 2) == core).astype(jnp.int32)
        half = jnp.where(back, 1 - own, own)
        start = jnp.where(
            away == 0,
            entries - 2 * CAP,
            jnp.where(away == far, 0, 2 * CAP + (far - 1 - distance) * 4 * CAP + jnp.where(back, 2 * CAP, 0)),
        )
        at = start + half * CAP + turn
        table[0, at] = n
        table[1, at] = slot_ref[row, k]
        return 0

    lax.fori_loop(0, blk * deps, enter, 0)


def place_kernel(chips, owner_ref, slot_ref, w_ref, cols_ref, p_ref, q_ref, table, x_sc, count):
    @pl.when(pl.program_id(0) == 0)
    def _():
        fill_table(chips, owner_ref, slot_ref, table, count)

    deps, points, cols = cols_ref.shape
    place = lax.broadcasted_iota(jnp.int32, (SPAN, LANES), 0).astype(jnp.float32).astype(jnp.bfloat16)
    q_ref[...] = jnp.zeros_like(q_ref)
    for k in range(deps):
        d = cols_ref[k]
        rel = ((d - d[0:1] + cols // 2) & (cols - 1)) - cols // 2
        low = jnp.min(rel, axis=0, keepdims=True)
        base = (d[0:1] + low) & (cols - 1)
        x_sc[k] = (rel - low + (base & (WIN - 1))).astype(jnp.float32).astype(jnp.bfloat16)
        q_ref[0, k:k + 1, :] = base // WIN
        for t in range(cols // LANES):
            part = slice(t * LANES, (t + 1) * LANES)
            x, w = x_sc[k, :, part], w_ref[k, :, part]
            acc = jnp.zeros((SPAN, LANES), jnp.bfloat16)
            for s in range(points):
                acc = jnp.where(place == x[s:s + 1], w[s:s + 1], acc)
            p_ref[k, :, part] = acc


def placed(chips, dep_owner, dep_slot, weight, places):
    blk, deps = dep_owner.shape
    items, points, cols = weight.shape
    entries = sum(stage_sizes(chips // 2))
    smem = pl.BlockSpec(memory_space=pltpu.SMEM)
    return pl.pallas_call(
        functools.partial(place_kernel, chips),
        grid=(blk,),
        in_specs=[
            smem,
            smem,
            pl.BlockSpec((deps, points, cols), lambda a: (a, 0, 0)),
            pl.BlockSpec((deps, points, cols), lambda a: (a, 0, 0)),
        ],
        out_specs=[
            pl.BlockSpec((deps, SPAN, cols), lambda a: (a, 0, 0)),
            pl.BlockSpec((1, 8, cols), lambda a: (a, 0, 0)),
            smem,
        ],
        out_shape=[
            jax.ShapeDtypeStruct((items, SPAN, cols), jnp.bfloat16),
            jax.ShapeDtypeStruct((blk, 8, cols), jnp.int32),
            jax.ShapeDtypeStruct((2, entries), jnp.int32),
        ],
        scratch_shapes=[
            pltpu.VMEM((deps, points, cols), jnp.bfloat16),
            pltpu.SMEM((2 * chips,), jnp.int32),
        ],
        compiler_params=pltpu.CompilerParams(
            dimension_semantics=("arbitrary",), vmem_limit_bytes=8 * MIB
        ),
        cost_estimate=pl.CostEstimate(flops=10000000000, bytes_accessed=5000000, transcendentals=0),
        name="place",
    )(dep_owner, dep_slot, weight, places)


def item_contribution(v, q, p_ref, index, v_sc, p_sc):
    rows, cols = v.shape
    for i in range(cols // WIN):
        v_sc[i * rows:(i + 1) * rows, :] = jnp.where(q == i, v, 0.0).astype(jnp.bfloat16)
    p_sc[0:SPAN, :] = p_ref[index]
    u = lax.dot_general(
        v_sc[...], p_sc[...], (((1,), (1,)), ((), ())), preferred_element_type=jnp.float32
    )
    lane = lax.broadcasted_iota(jnp.int32, (rows, LANES), 1)
    kept, passed = [], []
    for t in range(cols // LANES):
        u0, u1, u2, u3 = (u[(4 * t + j) * rows:(4 * t + j + 1) * rows] for j in range(4))
        kept.append(u0 + pltpu.roll(u1, WIN, 1))
        passed.append(pltpu.roll(u2, 2 * WIN, 1) + pltpu.roll(u3, 3 * WIN, 1))
    return [
        kept[t] + jnp.where(lane >= LANES // 2, passed[t], passed[t - 1]) for t in range(len(kept))
    ]


def stage_kernel(offset, listed, deps, rows, table, v_ref, p_ref, q_ref, *rest):
    outs, (v_sc, p_sc) = rest[:-2], rest[-2:]
    cols = v_ref.shape[-1]
    blk = v_ref.shape[0]
    p_sc[SPAN:, :] = jnp.zeros((LANES - SPAN, cols), jnp.bfloat16)
    for g, out in enumerate(outs):
        first = offset + g * 2 * CAP
        out[...] = jnp.zeros_like(out)
        if listed:
            ids = lax.broadcasted_iota(jnp.int32, (8, cols), 0)
            slots = jnp.zeros((8, cols), jnp.int32)
            for n in range(2 * CAP):
                slots = jnp.where(ids == n, table[1, first + n], slots)
            out[2 * CAP * rows:, :] = slots.astype(jnp.float32)

        def one(n, _):
            index = table[0, first + n]

            @pl.when(index >= 0)
            def _():
                row = lax.div(index, deps)
                v = v_ref[row].astype(jnp.float32)
                q = q_ref[row, pl.ds(lax.rem(index, deps), 1), :]
                parts = item_contribution(v, q, p_ref, index, v_sc, p_sc)
                if listed:
                    at = n * rows
                else:
                    at = (lax.div(n, CAP) * blk + table[1, first + n]) * rows
                at = pl.multiple_of(at, rows)
                for t, part in enumerate(parts):
                    where = (pl.ds(at, rows), slice(t * LANES, (t + 1) * LANES))
                    out[where] = out[where] + part

            return 0

        lax.fori_loop(0, 2 * CAP, one, 0)


def stage(offset, groups, listed, deps, table, v, p, q):
    blk, rows, cols = v.shape
    height = 2 * CAP * rows + 8 if listed else 2 * blk * rows
    vmem = pl.BlockSpec(memory_space=pltpu.VMEM)
    return pl.pallas_call(
        functools.partial(stage_kernel, offset, listed, deps, rows),
        in_specs=[pl.BlockSpec(memory_space=pltpu.SMEM), vmem, vmem, vmem],
        out_specs=[vmem] * groups,
        out_shape=[jax.ShapeDtypeStruct((height, cols), jnp.float32)] * groups,
        scratch_shapes=[
            pltpu.VMEM((cols // WIN * rows, cols), jnp.bfloat16),
            pltpu.VMEM((LANES, cols), jnp.bfloat16),
        ],
        compiler_params=pltpu.CompilerParams(vmem_limit_bytes=10 * MIB),
        cost_estimate=pl.CostEstimate(
            flops=groups * 1700000000, bytes_accessed=500000, transcendentals=0
        ),
        name="stage",
    )(table, v, p, q)


def merge_kernel(blk, rows, own_ref, given_ref, items_ref, *outs):
    width = own_ref.shape[1]
    for half, out in enumerate(outs):
        for c in range(0, width, LANES):
            part = slice(c, c + LANES)
            items = []
            for n in range(half * CAP, half * CAP + CAP):
                at = 2 * CAP * rows + n
                items.append((items_ref[at:at + 1, part], items_ref[n * rows:(n + 1) * rows, part]))
            for b in range(blk):
                at = (half * blk + b) * rows
                total = own_ref[at:at + rows, part] + given_ref[at:at + rows, part]
                for slot, value in items:
                    total = total + jnp.where(slot == float(b), value, 0.0)
                out[b * rows:(b + 1) * rows, part] = total


def merge(blk, rows, own, given, items):
    width = own.shape[1]
    return pl.pallas_call(
        functools.partial(merge_kernel, blk, rows),
        out_shape=[jax.ShapeDtypeStruct((blk * rows, width), jnp.float32)] * 2,
        compiler_params=pltpu.CompilerParams(vmem_limit_bytes=4 * MIB),
        cost_estimate=pl.CostEstimate(flops=1000000, bytes_accessed=1000000, transcendentals=0),
        name="merge",
    )(own, given, items)


def shards(adj_arrival, vert_coef, stencil_weight, stencil_cols, dep_owner, dep_slot):
    lev_dev, fields, blk, cols = adj_arrival.shape
    tiles, levels = lax.axis_size("tile"), lax.axis_size("lev")
    deps, points = stencil_weight.shape[1:3]
    items, rows = blk * deps, lev_dev * fields
    chips = tiles // 2
    far = chips // 2

    first = vert_coef[0, :1, None] * adj_arrival[:1]
    last = vert_coef[2, -1:, None] * adj_arrival[-1:]
    after = lax.ppermute(first, "lev", [(i + 1, i) for i in range(levels - 1)])
    before = lax.ppermute(last, "lev", [(i, i + 1) for i in range(levels - 1)])

    p, q, table = placed(
        chips,
        dep_owner,
        dep_slot,
        stencil_weight.reshape(items, points, cols),
        stencil_cols.reshape(items, points, cols),
    )

    z_low = vert_coef[0, 1:, None] * adj_arrival[1:]
    z_high = vert_coef[2, :-1, None] * adj_arrival[:-1]
    vert_adj = (
        jnp.concatenate([z_low, after], 0)
        + vert_coef[1][:, None] * adj_arrival
        + jnp.concatenate([before, z_high], 0)
    )
    vert_low = vert_adj.astype(jnp.bfloat16).reshape(rows, blk, cols)
    v = jnp.transpose(vert_low, (1, 0, 2))

    sibling = [(t, t ^ 1) for t in range(tiles)]
    ring = [(t, (t + 2 * (1 - 2 * (t % 2))) % tiles) for t in range(tiles)]
    size = blk * rows
    quad = 2 * CAP

    def made(table, at, groups, listed=False):
        return stage(at, groups, listed, deps, table, v, p, q)

    def behind(table, *values):
        return lax.optimization_barrier((table, *values))

    (others,) = made(table, 2 * quad, 1)
    table, others = behind(table, others)
    given = lax.ppermute(others, "tile", sibling)
    (farthest,) = made(table, 0, 1, True)
    table, farthest = behind(table, farthest)
    arrived = lax.ppermute(farthest, "tile", ring)
    (own,) = made(table, quad, 1)
    table, own = behind(table, own)
    totals = list(merge(blk, rows, own, given, arrived))
    for n in range(1, far - 1):
        own, others = made(table, quad + n * 2 * quad, 2)
        table, totals[0] = behind(table, totals[0])
        given = lax.ppermute(others, "tile", sibling)
        here = lax.optimization_barrier([own[:size] + given[:size], own[size:] + given[size:]])
        sums = [lax.ppermute(total, "tile", ring) for total in totals]
        totals = [total + mine for total, mine in zip(sums, here)]
    sums = [lax.ppermute(total, "tile", ring) for total in totals]
    (here,) = made(table, quad + (far - 1) * 2 * quad, 1)
    swapped = lax.ppermute(sums[0] + here[:size], "tile", sibling)
    result = sums[1] + here[size:] + swapped
    result = jnp.transpose(result.reshape(blk, rows, cols), (1, 0, 2))
    return result.reshape(lev_dev, fields, blk, cols)


def solution(mesh):
    in_specs = (
        P("lev", None, "tile", None),
        P(None, "lev", "tile", None),
        P("tile", None, None, None),
        P("tile", None, None, None),
        P("tile", None),
        P("tile", None),
    )
    out_specs = P("lev", None, "tile", None)
    return jax.shard_map(shards, mesh=mesh, in_specs=in_specs, out_specs=out_specs, check_vma=False)
```

```python
import functools

import jax
import jax.numpy as jnp
from jax import lax
from jax.experimental import pallas as pl
from jax.experimental.pallas import tpu as pltpu
from jax.sharding import PartitionSpec as P

WIN = 32
SPAN = 96
LANES = 128
CAP = 2
MIB = 1024 * 1024


def stage_sizes(far):
    return [2 * CAP] + [4 * CAP] * (far - 1) + [2 * CAP]


def fill_table(chips, owner_ref, slot_ref, table, count):
    deps, blk = owner_ref.shape
    far = chips // 2
    tile = lax.axis_index("tile")
    chip, core = lax.div(tile, 2), lax.rem(tile, 2)
    ahead = 1 - 2 * core
    entries = sum(stage_sizes(far))

    def clear(n, _):
        table[0, n] = jnp.int32(-1)
        table[1, n] = jnp.int32(0)
        return 0

    lax.fori_loop(0, entries, clear, 0)

    def reset(n, _):
        count[n] = jnp.int32(0)
        return 0

    lax.fori_loop(0, 2 * chips, reset, 0)

    def enter(n, _):
        row, k = lax.div(n, deps), lax.rem(n, deps)
        owner = owner_ref[k, row]
        turn = count[owner]
        count[owner] = turn + 1
        away = lax.rem(ahead * (lax.div(owner, 2) - chip) + chips, chips)
        back = away > far
        distance = jnp.where(back, chips - away, away)
        own = (lax.rem(owner, 2) == core).astype(jnp.int32)
        half = jnp.where(back, 1 - own, own)
        start = jnp.where(
            away == 0,
            entries - 2 * CAP,
            jnp.where(away == far, 0, 2 * CAP + (far - 1 - distance) * 4 * CAP + jnp.where(back, 2 * CAP, 0)),
        )
        at = start + half * CAP + turn
        table[0, at] = n
        table[1, at] = slot_ref[k, row]
        return 0

    lax.fori_loop(0, blk * deps, enter, 0)


def place_kernel(chips, deps, owner_ref, slot_ref, w_hbm, cols_hbm, p_ref, q_ref, table, w_sc, cols_sc, x_sc, count, sems):
    items, points, cols = cols_hbm.shape

    def fetches(a):
        part = pl.ds(a * deps, deps)
        return (
            pltpu.make_async_copy(w_hbm.at[part], w_sc.at[part], sems.at[0, a]),
            pltpu.make_async_copy(cols_hbm.at[part], cols_sc.at[part], sems.at[1, a]),
        )

    for a in range(items // deps):
        for fetch in fetches(a):
            fetch.start()
    fill_table(chips, owner_ref, slot_ref, table, count)
    q_ref[...] = jnp.zeros_like(q_ref)
    place = lax.broadcasted_iota(jnp.int32, (SPAN, LANES), 0).astype(jnp.float32).astype(jnp.bfloat16)

    def block(a, _):
        for fetch in fetches(a):
            fetch.wait()
        for k in range(deps):
            item = a * deps + k
            d = cols_sc[item]
            rel = ((d - d[0:1] + cols // 2) & (cols - 1)) - cols // 2
            low = jnp.min(rel, axis=0, keepdims=True)
            base = (d[0:1] + low) & (cols - 1)
            x_sc[k] = (rel - low + (base & (WIN - 1))).astype(jnp.float32).astype(jnp.bfloat16)
            q_ref[a, k:k + 1, :] = base // WIN
            for t in range(cols // LANES):
                part = slice(t * LANES, (t + 1) * LANES)
                x, w = x_sc[k, :, part], w_sc[item, :, part]
                acc = jnp.zeros((SPAN, LANES), jnp.bfloat16)
                for s in range(points):
                    acc = jnp.where(place == x[s:s + 1], w[s:s + 1], acc)
                p_ref[item, :, part] = acc
        return 0

    lax.fori_loop(0, items // deps, block, 0)


def placed(chips, dep_owner, dep_slot, weight, places):
    blk, deps = dep_owner.shape
    items, points, cols = weight.shape
    entries = sum(stage_sizes(chips // 2))
    smem = pl.BlockSpec(memory_space=pltpu.SMEM)
    vmem = pl.BlockSpec(memory_space=pltpu.VMEM)
    hbm = pl.BlockSpec(memory_space=pltpu.HBM)
    return pl.pallas_call(
        functools.partial(place_kernel, chips, deps),
        in_specs=[smem, smem, hbm, hbm],
        out_specs=[vmem, vmem, smem],
        out_shape=[
            jax.ShapeDtypeStruct((items, SPAN, cols), jnp.bfloat16),
            jax.ShapeDtypeStruct((blk, 8, cols), jnp.int32),
            jax.ShapeDtypeStruct((2, entries), jnp.int32),
        ],
        scratch_shapes=[
            pltpu.VMEM((items, points, cols), jnp.bfloat16),
            pltpu.VMEM((items, points, cols), jnp.int32),
            pltpu.VMEM((deps, points, cols), jnp.bfloat16),
            pltpu.SMEM((2 * chips,), jnp.int32),
            pltpu.SemaphoreType.DMA((2, blk)),
        ],
        compiler_params=pltpu.CompilerParams(vmem_limit_bytes=8 * MIB),
        cost_estimate=pl.CostEstimate(flops=10000000000, bytes_accessed=5000000, transcendentals=0),
        name="place",
    )(dep_owner.T, dep_slot.T, weight, places)


def item_contribution(v, q, p_ref, index, v_sc, p_sc):
    rows, cols = v.shape
    for i in range(cols // WIN):
        v_sc[i * rows:(i + 1) * rows, :] = jnp.where(q == i, v, 0.0).astype(jnp.bfloat16)
    p_sc[0:SPAN, :] = p_ref[index]
    u = lax.dot_general(
        v_sc[...], p_sc[...], (((1,), (1,)), ((), ())), preferred_element_type=jnp.float32
    )
    lane = lax.broadcasted_iota(jnp.int32, (rows, LANES), 1)
    kept, passed = [], []
    for t in range(cols // LANES):
        u0, u1, u2, u3 = (u[(4 * t + j) * rows:(4 * t + j + 1) * rows] for j in range(4))
        kept.append(u0 + pltpu.roll(u1, WIN, 1))
        passed.append(pltpu.roll(u2, 2 * WIN, 1) + pltpu.roll(u3, 3 * WIN, 1))
    return [
        kept[t] + jnp.where(lane >= LANES // 2, passed[t], passed[t - 1]) for t in range(len(kept))
    ]


def stage_kernel(groups, deps, rows, table, v_ref, p_ref, q_ref, *rest):
    outs, (v_sc, p_sc) = rest[:-2], rest[-2:]
    cols = v_ref.shape[-1]
    blk = v_ref.shape[0]
    p_sc[SPAN:, :] = jnp.zeros((LANES - SPAN, cols), jnp.bfloat16)
    for (first, listed), out in zip(groups, outs):
        out[...] = jnp.zeros_like(out)
        if listed:
            ids = lax.broadcasted_iota(jnp.int32, (8, cols), 0)
            slots = jnp.zeros((8, cols), jnp.int32)
            for n in range(2 * CAP):
                slots = jnp.where(ids == n, table[1, first + n], slots)
            out[2 * CAP * rows:, :] = slots.astype(jnp.float32)

        def one(n, _):
            index = table[0, first + n]

            @pl.when(index >= 0)
            def _():
                row = lax.div(index, deps)
                v = v_ref[row].astype(jnp.float32)
                q = q_ref[row, pl.ds(lax.rem(index, deps), 1), :]
                parts = item_contribution(v, q, p_ref, index, v_sc, p_sc)
                if listed:
                    at = n * rows
                else:
                    at = (lax.div(n, CAP) * blk + table[1, first + n]) * rows
                at = pl.multiple_of(at, rows)
                for t, part in enumerate(parts):
                    where = (pl.ds(at, rows), slice(t * LANES, (t + 1) * LANES))
                    out[where] = out[where] + part

            return 0

        lax.fori_loop(0, 2 * CAP, one, 0)


def stage(groups, deps, table, v, p, q):
    blk, rows, cols = v.shape
    heights = [2 * CAP * rows + 8 if listed else 2 * blk * rows for _, listed in groups]
    vmem = pl.BlockSpec(memory_space=pltpu.VMEM)
    return pl.pallas_call(
        functools.partial(stage_kernel, groups, deps, rows),
        in_specs=[pl.BlockSpec(memory_space=pltpu.SMEM), vmem, vmem, vmem],
        out_specs=[vmem] * len(groups),
        out_shape=[jax.ShapeDtypeStruct((height, cols), jnp.float32) for height in heights],
        scratch_shapes=[
            pltpu.VMEM((cols // WIN * rows, cols), jnp.bfloat16),
            pltpu.VMEM((LANES, cols), jnp.bfloat16),
        ],
        compiler_params=pltpu.CompilerParams(vmem_limit_bytes=10 * MIB),
        cost_estimate=pl.CostEstimate(
            flops=len(groups) * 1700000000, bytes_accessed=500000, transcendentals=0
        ),
        name="stage",
    )(table, v, p, q)


def merge_kernel(blk, rows, dense_ref, *refs):
    lists, outs = refs[:-2], refs[-2:]
    width = dense_ref.shape[1]
    for half, out in enumerate(outs):
        for c in range(0, width, LANES):
            part = slice(c, c + LANES)
            items = []
            for ref in lists:
                for n in range(half * CAP, half * CAP + CAP):
                    at = 2 * CAP * rows + n
                    items.append((ref[at:at + 1, part], ref[n * rows:(n + 1) * rows, part]))
            for b in range(blk):
                at = (half * blk + b) * rows
                total = dense_ref[at:at + rows, part]
                for slot, value in items:
                    total = total + jnp.where(slot == float(b), value, 0.0)
                out[b * rows:(b + 1) * rows, part] = total


def merge(blk, rows, dense, *lists):
    width = dense.shape[1]
    return list(pl.pallas_call(
        functools.partial(merge_kernel, blk, rows),
        out_shape=[jax.ShapeDtypeStruct((blk * rows, width), jnp.float32)] * 2,
        compiler_params=pltpu.CompilerParams(vmem_limit_bytes=6 * MIB),
        cost_estimate=pl.CostEstimate(flops=1000000, bytes_accessed=1000000, transcendentals=0),
        name="merge",
    )(dense, *lists))


def edges_kernel(adj0_ref, coef0_ref, adj1_ref, coef1_ref, first_ref, last_ref):
    first_ref[0] = coef0_ref[0] * adj0_ref[0]
    last_ref[0] = coef1_ref[0] * adj1_ref[0]


def edges(adj, coef):
    lev, fields, blk, cols = adj.shape
    shape = (1, fields, blk, cols)
    return pl.pallas_call(
        edges_kernel,
        grid=(1,),
        in_specs=[
            pl.BlockSpec(shape, lambda i: (0, 0, 0, 0)),
            pl.BlockSpec((1, 1, blk, cols), lambda i: (0, 0, 0, 0)),
            pl.BlockSpec(shape, lambda i: (lev - 1, 0, 0, 0)),
            pl.BlockSpec((1, 1, blk, cols), lambda i: (2, lev - 1, 0, 0)),
        ],
        out_specs=[pl.BlockSpec(shape, lambda i: (0, 0, 0, 0))] * 2,
        out_shape=[jax.ShapeDtypeStruct(shape, jnp.float32)] * 2,
        compiler_params=pltpu.CompilerParams(vmem_limit_bytes=60 * MIB),
        name="edges",
    )(adj, coef, adj, coef)


def vertical_kernel(adj_ref, coef_ref, after_ref, before_ref, v_ref):
    lev, fields, blk, cols = adj_ref.shape
    for c in range(0, cols, LANES):
        part = slice(c, c + LANES)
        levels = []
        for m in range(lev):
            low = after_ref[0, :, :, part] if m == lev - 1 else coef_ref[0, m + 1, :, part] * adj_ref[m + 1, :, :, part]
            high = before_ref[0, :, :, part] if m == 0 else coef_ref[2, m - 1, :, part] * adj_ref[m - 1, :, :, part]
            levels.append(low + coef_ref[1, m, :, part] * adj_ref[m, :, :, part] + high)
        whole = jnp.concatenate(levels, 0)
        v_ref[:, :, part] = jnp.swapaxes(whole, 0, 1).astype(jnp.bfloat16)


def vertical(adj, coef, after, before):
    lev, fields, blk, cols = adj.shape
    return pl.pallas_call(
        vertical_kernel,
        out_shape=jax.ShapeDtypeStruct((blk, lev * fields, cols), jnp.bfloat16),
        compiler_params=pltpu.CompilerParams(vmem_limit_bytes=4 * MIB),
        cost_estimate=pl.CostEstimate(flops=1000000, bytes_accessed=1000000, transcendentals=0),
        name="vertical",
    )(adj, coef, after, before)


def shards(adj_arrival, vert_coef, stencil_weight, stencil_cols, dep_owner, dep_slot):
    lev_dev, fields, blk, cols = adj_arrival.shape
    tiles, levels = lax.axis_size("tile"), lax.axis_size("lev")
    deps, points = stencil_weight.shape[1:3]
    items, rows = blk * deps, lev_dev * fields
    chips = tiles // 2
    far = chips // 2

    first, last = edges(adj_arrival, vert_coef)
    after = lax.ppermute(first, "lev", [(i + 1, i) for i in range(levels - 1)])
    before = lax.ppermute(last, "lev", [(i, i + 1) for i in range(levels - 1)])

    p, q, table = placed(
        chips,
        dep_owner,
        dep_slot,
        stencil_weight.reshape(items, points, cols),
        stencil_cols.reshape(items, points, cols),
    )

    v = vertical(adj_arrival, vert_coef, after, before)

    sibling = [(t, t ^ 1) for t in range(tiles)]
    ring = [(t, (t + 2 * (1 - 2 * (t % 2))) % tiles) for t in range(tiles)]
    quad = 2 * CAP

    def made(table, *groups):
        return stage(groups, deps, table, v, p, q)

    def behind(table, value):
        return lax.optimization_barrier((table, value))

    def onward(values, pairs):
        return [lax.ppermute(value, "tile", pairs) for value in values]

    own, others = made(table, (quad, True), (2 * quad, True))
    given = lax.ppermute(others, "tile", sibling)
    table, given = behind(table, given)
    arrived = onward([own, given], ring)
    opposite = None
    for h in range(far - 2, 0, -1):
        at = quad + (far - 1 - h) * 2 * quad
        own, others = made(table, (at, False), (at + quad, True))
        given = lax.ppermute(others, "tile", sibling)
        if h == far - 2:
            totals = merge(blk, rows, own, given, *arrived)
        else:
            totals = [total + mine for total, mine in zip(sums, lax.optimization_barrier(merge(blk, rows, own, given)))]
        table, totals[0] = behind(table, totals[0])
        if h == far - 3:
            (listed,) = made(table, (0, True))
            opposite = lax.ppermute(listed, "tile", [(t, (t + tiles // 2) % tiles) for t in range(tiles)])
        sums = onward(totals, ring)
    (here,) = made(table, (quad + (far - 1) * 2 * quad, False))
    here = lax.optimization_barrier(merge(blk, rows, here, opposite))
    swapped = lax.ppermute(sums[0] + here[0], "tile", sibling)
    result = sums[1] + here[1] + swapped
    result = jnp.transpose(result.reshape(blk, rows, cols), (1, 0, 2))
    return result.reshape(lev_dev, fields, blk, cols)


def solution(mesh):
    in_specs = (
        P("lev", None, "tile", None),
        P(None, "lev", "tile", None),
        P("tile", None, None, None),
        P("tile", None, None, None),
        P("tile", None),
        P("tile", None),
    )
    out_specs = P("lev", None, "tile", None)
    return jax.shard_map(shards, mesh=mesh, in_specs=in_specs, out_specs=out_specs, check_vma=False)
```

```python
import functools

import jax
import jax.numpy as jnp
from jax import lax
from jax.experimental import pallas as pl
from jax.experimental.pallas import tpu as pltpu
from jax.sharding import PartitionSpec as P

WIN = 32
SPAN = 96
LANES = 128
TILE = 16
CAP = 2
MIB = 1024 * 1024


def stage_sizes(far):
    return [2 * CAP] + [4 * CAP] * (far - 1) + [2 * CAP]


def fill_table(chips, owner_ref, slot_ref, table, count):
    deps, blk = owner_ref.shape
    far = chips // 2
    tile = lax.axis_index("tile")
    chip, core = lax.div(tile, 2), lax.rem(tile, 2)
    ahead = 1 - 2 * core
    entries = sum(stage_sizes(far))

    def clear(n, _):
        table[0, n] = jnp.int32(-1)
        table[1, n] = jnp.int32(0)
        return 0

    lax.fori_loop(0, entries, clear, 0)

    def reset(n, _):
        count[n] = jnp.int32(0)
        return 0

    lax.fori_loop(0, 2 * chips, reset, 0)

    def enter(n, _):
        row, k = lax.div(n, deps), lax.rem(n, deps)
        owner = owner_ref[k, row]
        turn = count[owner]
        count[owner] = turn + 1
        away = lax.rem(ahead * (lax.div(owner, 2) - chip) + chips, chips)
        back = away > far
        distance = jnp.where(back, chips - away, away)
        own = (lax.rem(owner, 2) == core).astype(jnp.int32)
        half = jnp.where(back, 1 - own, own)
        start = jnp.where(
            away == 0,
            entries - 2 * CAP,
            jnp.where(away == far, 0, 2 * CAP + (far - 1 - distance) * 4 * CAP + jnp.where(back, 2 * CAP, 0)),
        )
        at = start + half * CAP + turn
        table[0, at] = n
        table[1, at] = slot_ref[k, row]
        return 0

    lax.fori_loop(0, blk * deps, enter, 0)


def place_kernel(chips, deps, owner_ref, slot_ref, w_ref, cols_ref, p_ref, q_ref, table, x_sc, w_sc, count):
    items, points, cols = cols_ref.shape
    fill_table(chips, owner_ref, slot_ref, table, count)
    q_ref[...] = jnp.zeros_like(q_ref)
    first = lax.broadcasted_iota(jnp.int32, (TILE, LANES), 0)
    places = [(first + i).astype(jnp.float32).astype(jnp.bfloat16) for i in range(0, SPAN, TILE)]

    def block(a, _):
        for k in range(deps):
            item = a * deps + k
            d = cols_ref[item]
            rel = ((d - d[0:1] + cols // 2) & (cols - 1)) - cols // 2
            low = jnp.min(rel, axis=0, keepdims=True)
            base = (d[0:1] + low) & (cols - 1)
            x_sc[k] = (rel - low + (base & (WIN - 1))).astype(jnp.float32)
            w_sc[k] = w_ref[item].astype(jnp.float32)
            q_ref[a, k:k + 1, :] = base // WIN
            for t in range(cols // LANES):
                part = slice(t * LANES, (t + 1) * LANES)
                acc = [jnp.zeros((TILE, LANES), jnp.bfloat16)] * len(places)
                for s in range(points):
                    x = jnp.broadcast_to(x_sc[k, s:s + 1, part], (TILE, LANES)).astype(jnp.bfloat16)
                    w = jnp.broadcast_to(w_sc[k, s:s + 1, part], (TILE, LANES)).astype(jnp.bfloat16)
                    acc = [jnp.where(place == x, w, total) for place, total in zip(places, acc)]
                for i, total in enumerate(acc):
                    p_ref[item, i * TILE:(i + 1) * TILE, part] = total
        return 0

    lax.fori_loop(0, items // deps, block, 0)


def placed(chips, dep_owner, dep_slot, weight, places):
    blk, deps = dep_owner.shape
    items, points, cols = weight.shape
    entries = sum(stage_sizes(chips // 2))
    smem = pl.BlockSpec(memory_space=pltpu.SMEM)
    vmem = pl.BlockSpec(memory_space=pltpu.VMEM)
    return pl.pallas_call(
        functools.partial(place_kernel, chips, deps),
        in_specs=[smem, smem, vmem, vmem],
        out_specs=[vmem, vmem, smem],
        out_shape=[
            jax.ShapeDtypeStruct((items, SPAN, cols), jnp.bfloat16),
            jax.ShapeDtypeStruct((blk, 8, cols), jnp.int32),
            jax.ShapeDtypeStruct((2, entries), jnp.int32),
        ],
        scratch_shapes=[
            pltpu.VMEM((deps, points, cols), jnp.float32),
            pltpu.VMEM((deps, points, cols), jnp.float32),
            pltpu.SMEM((2 * chips,), jnp.int32),
        ],
        compiler_params=pltpu.CompilerParams(vmem_limit_bytes=8 * MIB),
        cost_estimate=pl.CostEstimate(flops=10000000000, bytes_accessed=5000000, transcendentals=0),
        name="place",
    )(dep_owner.T, dep_slot.T, weight, places)


def item_contribution(v, q, p_ref, index, v_sc):
    rows, cols = v.shape
    window = jnp.broadcast_to(q.astype(jnp.float32), (rows, cols)).astype(jnp.bfloat16)
    for i in range(cols // WIN):
        v_sc[i * rows:(i + 1) * rows, :] = jnp.where(window == jnp.bfloat16(i), v, jnp.bfloat16(0))
    u = lax.dot_general(
        v_sc[...], p_ref[index], (((1,), (1,)), ((), ())), preferred_element_type=jnp.float32
    )
    u = jnp.concatenate([u, jnp.zeros((u.shape[0], LANES - SPAN), jnp.float32)], 1)
    lane = lax.broadcasted_iota(jnp.int32, (rows, LANES), 1)
    kept, passed = [], []
    for t in range(cols // LANES):
        u0, u1, u2, u3 = (u[(4 * t + j) * rows:(4 * t + j + 1) * rows] for j in range(4))
        kept.append(u0 + pltpu.roll(u1, WIN, 1))
        passed.append(pltpu.roll(u2, 2 * WIN, 1) + pltpu.roll(u3, 3 * WIN, 1))
    return [
        kept[t] + jnp.where(lane >= LANES // 2, passed[t], passed[t - 1]) for t in range(len(kept))
    ]


def stage_kernel(groups, deps, rows, table, v_ref, p_ref, q_ref, *rest):
    *outs, v_sc = rest
    cols = v_ref.shape[-1]
    blk = v_ref.shape[0]
    for (firsts, listed), out in zip(groups, outs):
        out[...] = jnp.zeros_like(out)
        for number, first in enumerate(firsts):
            top = number * (2 * CAP * rows + 8)
            if listed:
                ids = lax.broadcasted_iota(jnp.int32, (8, cols), 0)
                slots = jnp.zeros((8, cols), jnp.int32)
                for n in range(2 * CAP):
                    slots = jnp.where(ids == n, table[1, first + n], slots)
                out[top + 2 * CAP * rows:top + 2 * CAP * rows + 8, :] = slots.astype(jnp.float32)

            def one(n, _):
                index = table[0, first + n]

                @pl.when(index >= 0)
                def _():
                    row = lax.div(index, deps)
                    q = q_ref[row, pl.ds(lax.rem(index, deps), 1), :]
                    parts = item_contribution(v_ref[row], q, p_ref, index, v_sc)
                    if listed:
                        at = pl.multiple_of(top + n * rows, 8)
                    else:
                        at = pl.multiple_of((lax.div(n, CAP) * blk + table[1, first + n]) * rows, rows)
                    for t, part in enumerate(parts):
                        where = (pl.ds(at, rows), slice(t * LANES, (t + 1) * LANES))
                        out[where] = out[where] + part

                return 0

            lax.fori_loop(0, 2 * CAP, one, 0)


def stage(groups, deps, table, v, p, q):
    blk, rows, cols = v.shape
    heights = [len(firsts) * (2 * CAP * rows + 8) if listed else 2 * blk * rows for firsts, listed in groups]
    vmem = pl.BlockSpec(memory_space=pltpu.VMEM)
    return pl.pallas_call(
        functools.partial(stage_kernel, groups, deps, rows),
        in_specs=[pl.BlockSpec(memory_space=pltpu.SMEM), vmem, vmem, vmem],
        out_specs=[vmem] * len(groups),
        out_shape=[jax.ShapeDtypeStruct((height, cols), jnp.float32) for height in heights],
        scratch_shapes=[
            pltpu.VMEM((cols // WIN * rows, cols), jnp.bfloat16),
        ],
        compiler_params=pltpu.CompilerParams(vmem_limit_bytes=10 * MIB),
        cost_estimate=pl.CostEstimate(
            flops=len(groups) * 200000000, bytes_accessed=500000, transcendentals=0
        ),
        name="stage",
    )(table, v, p, q)


def merge_kernel(blk, rows, picks, dense_ref, *refs):
    lists, outs = refs[:-2], refs[-2:]
    width = dense_ref.shape[1]
    for half, out in enumerate(outs):
        for c in range(0, width, LANES):
            part = slice(c, c + LANES)
            items = []
            for ref, numbers in zip(lists, picks):
                for top in (number * (2 * CAP * rows + 8) for number in numbers):
                    for n in range(half * CAP, half * CAP + CAP):
                        at, slot = top + n * rows, top + 2 * CAP * rows + n
                        items.append((ref[slot:slot + 1, part], ref[at:at + rows, part]))
            for b in range(blk):
                at = (half * blk + b) * rows
                total = dense_ref[at:at + rows, part]
                for slot, value in items:
                    total = total + jnp.where(slot == float(b), value, 0.0)
                out[b * rows:(b + 1) * rows, part] = total


def merge(blk, rows, dense, *lists):
    width = dense.shape[1]
    return list(pl.pallas_call(
        functools.partial(merge_kernel, blk, rows, [numbers for _, numbers in lists]),
        out_shape=[jax.ShapeDtypeStruct((blk * rows, width), jnp.float32)] * 2,
        compiler_params=pltpu.CompilerParams(vmem_limit_bytes=6 * MIB),
        cost_estimate=pl.CostEstimate(flops=1000000, bytes_accessed=1000000, transcendentals=0),
        name="merge",
    )(dense, *(ref for ref, _ in lists)))


def edges_kernel(adj0_ref, coef0_ref, adj1_ref, coef1_ref, first_ref, last_ref):
    first_ref[0] = coef0_ref[0] * adj0_ref[0]
    last_ref[0] = coef1_ref[0] * adj1_ref[0]


def edges(adj, coef):
    lev, fields, blk, cols = adj.shape
    shape = (1, fields, blk, cols)
    return pl.pallas_call(
        edges_kernel,
        grid=(1,),
        in_specs=[
            pl.BlockSpec(shape, lambda i: (0, 0, 0, 0)),
            pl.BlockSpec((1, 1, blk, cols), lambda i: (0, 0, 0, 0)),
            pl.BlockSpec(shape, lambda i: (lev - 1, 0, 0, 0)),
            pl.BlockSpec((1, 1, blk, cols), lambda i: (2, lev - 1, 0, 0)),
        ],
        out_specs=[pl.BlockSpec(shape, lambda i: (0, 0, 0, 0))] * 2,
        out_shape=[jax.ShapeDtypeStruct(shape, jnp.float32)] * 2,
        compiler_params=pltpu.CompilerParams(vmem_limit_bytes=60 * MIB),
        name="edges",
    )(adj, coef, adj, coef)


def vertical_kernel(adj_ref, coef_ref, after_ref, before_ref, v_ref):
    lev, fields, blk, cols = adj_ref.shape
    for c in range(0, cols, LANES):
        part = slice(c, c + LANES)
        levels = []
        for m in range(lev):
            low = after_ref[0, :, :, part] if m == lev - 1 else coef_ref[0, m + 1, :, part] * adj_ref[m + 1, :, :, part]
            high = before_ref[0, :, :, part] if m == 0 else coef_ref[2, m - 1, :, part] * adj_ref[m - 1, :, :, part]
            levels.append(low + coef_ref[1, m, :, part] * adj_ref[m, :, :, part] + high)
        whole = jnp.concatenate(levels, 0)
        v_ref[:, :, part] = jnp.swapaxes(whole, 0, 1).astype(jnp.bfloat16)


def vertical(adj, coef, after, before):
    lev, fields, blk, cols = adj.shape
    return pl.pallas_call(
        vertical_kernel,
        out_shape=jax.ShapeDtypeStruct((blk, lev * fields, cols), jnp.bfloat16),
        compiler_params=pltpu.CompilerParams(vmem_limit_bytes=4 * MIB),
        cost_estimate=pl.CostEstimate(flops=1000000, bytes_accessed=1000000, transcendentals=0),
        name="vertical",
    )(adj, coef, after, before)


def shards(adj_arrival, vert_coef, stencil_weight, stencil_cols, dep_owner, dep_slot):
    lev_dev, fields, blk, cols = adj_arrival.shape
    tiles, levels = lax.axis_size("tile"), lax.axis_size("lev")
    deps, points = stencil_weight.shape[1:3]
    items, rows = blk * deps, lev_dev * fields
    chips = tiles // 2
    far = chips // 2

    first, last = edges(adj_arrival, vert_coef)
    after = lax.ppermute(first, "lev", [(i + 1, i) for i in range(levels - 1)])
    before = lax.ppermute(last, "lev", [(i, i + 1) for i in range(levels - 1)])

    p, q, table = placed(
        chips,
        dep_owner,
        dep_slot,
        stencil_weight.reshape(items, points, cols),
        stencil_cols.reshape(items, points, cols),
    )

    v = vertical(adj_arrival, vert_coef, after, before)

    sibling = [(t, t ^ 1) for t in range(tiles)]
    ring = [(t, (t + 2 * (1 - 2 * (t % 2))) % tiles) for t in range(tiles)]
    quad = 2 * CAP

    def made(table, *groups):
        return stage(groups, deps, table, v, p, q)

    def behind(table, value):
        return lax.optimization_barrier((table, value))

    def onward(values, pairs):
        return [lax.ppermute(value, "tile", pairs) for value in values]

    def own_at(h):
        return quad + (far - 1 - h) * 2 * quad

    def other_at(h):
        return own_at(h) + quad

    (listed,) = made(table, ((0,), True))
    table, listed = behind(table, listed)
    (farthest,) = onward([listed], ring)
    own, others = made(table, ((own_at(far - 1),), True), ((other_at(far - 1),), True))
    (given,) = onward([others], sibling)
    table, given = behind(table, given)
    arrived = onward([jnp.concatenate([own, farthest], 0), given], ring)

    totals, waiting = None, {}
    near = far - 2

    def exchanged(table, distances, *others):
        (listed,) = made(table, (tuple(other_at(d) for d in distances), True))
        table, listed, *others = lax.optimization_barrier((table, listed, *others))
        (given,) = onward([listed], sibling)
        waiting.update({d: (given, (number,)) for number, d in enumerate(distances)})
        return table, *others

    (table,) = exchanged(table, range(near, near // 2, -1))
    for h in range(near, 0, -1):
        (own,) = made(table, ((own_at(h),), False))
        if totals is None:
            table, own = behind(table, own)
            table, own = exchanged(table, range(near // 2, 0, -1), own)
            totals = merge(blk, rows, own, waiting[h], (arrived[0], (0, 1)), (arrived[1], (0,)))
        else:
            mine = lax.optimization_barrier(merge(blk, rows, own, waiting[h]))
            totals = [total + here for total, here in zip(onward(totals, ring), mine)]
        table, totals[0] = behind(table, totals[0])
    sums = onward(totals, ring)
    (here,) = made(table, ((own_at(0),), False))
    (swapped,) = onward([sums[0] + here[:blk * rows]], sibling)
    result = sums[1] + here[blk * rows:] + swapped
    result = jnp.transpose(result.reshape(blk, rows, cols), (1, 0, 2))
    return result.reshape(lev_dev, fields, blk, cols)


def solution(mesh):
    in_specs = (
        P("lev", None, "tile", None),
        P(None, "lev", "tile", None),
        P("tile", None, None, None),
        P("tile", None, None, None),
        P("tile", None),
        P("tile", None),
    )
    out_specs = P("lev", None, "tile", None)
    return jax.shard_map(shards, mesh=mesh, in_specs=in_specs, out_specs=out_specs, check_vma=False)
```

```python
import functools

import jax
import jax.numpy as jnp
from jax import lax
from jax.experimental import pallas as pl
from jax.experimental.pallas import tpu as pltpu
from jax.sharding import PartitionSpec as P

WIN = 32
SPAN = 96
LANES = 128
TILE = 16
CAP = 2
MIB = 1024 * 1024


def stage_sizes(far):
    return [2 * CAP] + [4 * CAP] * (far - 1) + [2 * CAP]


def fill_table(chips, pair_ref, table, count):
    deps, blk = pair_ref.shape[1:]
    far = chips // 2
    tile = lax.axis_index("tile")
    chip, core = lax.div(tile, 2), lax.rem(tile, 2)
    ahead = 1 - 2 * core
    entries = sum(stage_sizes(far))

    def clear(n, _):
        table[0, n] = jnp.int32(-1)
        table[1, n] = jnp.int32(0)
        return 0

    lax.fori_loop(0, entries, clear, 0)

    def reset(n, _):
        count[n] = jnp.int32(0)
        return 0

    lax.fori_loop(0, 2 * chips, reset, 0)

    def enter(n, _):
        row, k = lax.div(n, deps), lax.rem(n, deps)
        owner = pair_ref[0, k, row]
        turn = count[owner]
        count[owner] = turn + 1
        away = lax.rem(ahead * (lax.div(owner, 2) - chip) + chips, chips)
        back = away > far
        distance = jnp.where(back, chips - away, away)
        own = (lax.rem(owner, 2) == core).astype(jnp.int32)
        half = jnp.where(back, 1 - own, own)
        start = jnp.where(
            away == 0,
            entries - 2 * CAP,
            jnp.where(away == far, 0, 2 * CAP + (far - 1 - distance) * 4 * CAP + jnp.where(back, 2 * CAP, 0)),
        )
        at = start + half * CAP + turn
        table[0, at] = n
        table[1, at] = pair_ref[1, k, row]
        return 0

    lax.fori_loop(0, blk * deps, enter, 0)


def place_kernel(chips, deps, pair_ref, w_ref, cols_ref, p_ref, q_ref, table, x_sc, w_sc, count):
    items, points, cols = cols_ref.shape
    fill_table(chips, pair_ref, table, count)
    q_ref[...] = jnp.zeros_like(q_ref)
    first = lax.broadcasted_iota(jnp.int32, (TILE, LANES), 0)
    places = [(first + i).astype(jnp.float32).astype(jnp.bfloat16) for i in range(0, SPAN, TILE)]

    def block(a, _):
        for k in range(deps):
            item = a * deps + k
            d = cols_ref[item]
            rel = ((d - d[0:1] + cols // 2) & (cols - 1)) - cols // 2
            low = jnp.min(rel, axis=0, keepdims=True)
            base = (d[0:1] + low) & (cols - 1)
            x_sc[k] = (rel - low + (base & (WIN - 1))).astype(jnp.float32)
            w_sc[k] = w_ref[item].astype(jnp.float32)
            q_ref[a, k:k + 1, :] = base // WIN
            for t in range(cols // LANES):
                part = slice(t * LANES, (t + 1) * LANES)
                acc = [jnp.zeros((TILE, LANES), jnp.bfloat16)] * len(places)
                for s in range(points):
                    x = jnp.broadcast_to(x_sc[k, s:s + 1, part], (TILE, LANES)).astype(jnp.bfloat16)
                    w = jnp.broadcast_to(w_sc[k, s:s + 1, part], (TILE, LANES)).astype(jnp.bfloat16)
                    acc = [jnp.where(place == x, w, total) for place, total in zip(places, acc)]
                for i, total in enumerate(acc):
                    p_ref[item, i * TILE:(i + 1) * TILE, part] = total
        return 0

    lax.fori_loop(0, items // deps, block, 0)


def placed(chips, dep_owner, dep_slot, weight, places):
    blk, deps = dep_owner.shape
    items, points, cols = weight.shape
    entries = sum(stage_sizes(chips // 2))
    smem = pl.BlockSpec(memory_space=pltpu.SMEM)
    vmem = pl.BlockSpec(memory_space=pltpu.VMEM)
    return pl.pallas_call(
        functools.partial(place_kernel, chips, deps),
        in_specs=[smem, vmem, vmem],
        out_specs=[vmem, vmem, smem],
        out_shape=[
            jax.ShapeDtypeStruct((items, SPAN, cols), jnp.bfloat16),
            jax.ShapeDtypeStruct((blk, 8, cols), jnp.int32),
            jax.ShapeDtypeStruct((2, entries), jnp.int32),
        ],
        scratch_shapes=[
            pltpu.VMEM((deps, points, cols), jnp.float32),
            pltpu.VMEM((deps, points, cols), jnp.float32),
            pltpu.SMEM((2 * chips,), jnp.int32),
        ],
        compiler_params=pltpu.CompilerParams(vmem_limit_bytes=8 * MIB),
        cost_estimate=pl.CostEstimate(flops=10000000000, bytes_accessed=5000000, transcendentals=0),
        name="place",
    )(jnp.stack([dep_owner.T, dep_slot.T]), weight, places)


def item_contribution(v, q, p_ref, index, v_sc):
    rows, cols = v.shape
    window = jnp.broadcast_to(q.astype(jnp.float32), (rows, cols)).astype(jnp.bfloat16)
    for i in range(cols // WIN):
        v_sc[i * rows:(i + 1) * rows, :] = jnp.where(window == jnp.bfloat16(i), v, jnp.bfloat16(0))
    u = lax.dot_general(
        v_sc[...], p_ref[index], (((1,), (1,)), ((), ())), preferred_element_type=jnp.float32
    )
    u = jnp.concatenate([u, jnp.zeros((u.shape[0], LANES - SPAN), jnp.float32)], 1)
    lane = lax.broadcasted_iota(jnp.int32, (rows, LANES), 1)
    kept, passed = [], []
    for t in range(cols // LANES):
        u0, u1, u2, u3 = (u[(4 * t + j) * rows:(4 * t + j + 1) * rows] for j in range(4))
        kept.append(u0 + pltpu.roll(u1, WIN, 1))
        passed.append(pltpu.roll(u2, 2 * WIN, 1) + pltpu.roll(u3, 3 * WIN, 1))
    return [
        kept[t] + jnp.where(lane >= LANES // 2, passed[t], passed[t - 1]) for t in range(len(kept))
    ]


def stage_kernel(groups, deps, rows, table, v_ref, p_ref, q_ref, *rest):
    *outs, v_sc = rest
    cols = v_ref.shape[-1]
    blk = v_ref.shape[0]
    for (firsts, listed), out in zip(groups, outs):
        out[...] = jnp.zeros_like(out)
        for number, first in enumerate(firsts):
            top = number * (2 * CAP * rows + 8)
            if listed:
                ids = lax.broadcasted_iota(jnp.int32, (8, cols), 0)
                slots = jnp.zeros((8, cols), jnp.int32)
                for n in range(2 * CAP):
                    slots = jnp.where(ids == n, table[1, first + n], slots)
                out[top + 2 * CAP * rows:top + 2 * CAP * rows + 8, :] = slots.astype(jnp.float32)

            def one(n, _):
                index = table[0, first + n]

                @pl.when(index >= 0)
                def _():
                    row = lax.div(index, deps)
                    q = q_ref[row, pl.ds(lax.rem(index, deps), 1), :]
                    parts = item_contribution(v_ref[row], q, p_ref, index, v_sc)
                    if listed:
                        at = pl.multiple_of(top + n * rows, 8)
                    else:
                        at = pl.multiple_of((lax.div(n, CAP) * blk + table[1, first + n]) * rows, rows)
                    for t, part in enumerate(parts):
                        where = (pl.ds(at, rows), slice(t * LANES, (t + 1) * LANES))
                        out[where] = out[where] + part

                return 0

            lax.fori_loop(0, 2 * CAP, one, 0)


def stage(groups, deps, table, v, p, q):
    blk, rows, cols = v.shape
    heights = [len(firsts) * (2 * CAP * rows + 8) if listed else 2 * blk * rows for firsts, listed in groups]
    vmem = pl.BlockSpec(memory_space=pltpu.VMEM)
    return pl.pallas_call(
        functools.partial(stage_kernel, groups, deps, rows),
        in_specs=[pl.BlockSpec(memory_space=pltpu.SMEM), vmem, vmem, vmem],
        out_specs=[vmem] * len(groups),
        out_shape=[jax.ShapeDtypeStruct((height, cols), jnp.float32) for height in heights],
        scratch_shapes=[
            pltpu.VMEM((cols // WIN * rows, cols), jnp.bfloat16),
        ],
        compiler_params=pltpu.CompilerParams(vmem_limit_bytes=10 * MIB),
        cost_estimate=pl.CostEstimate(
            flops=len(groups) * 200000000, bytes_accessed=500000, transcendentals=0
        ),
        name="stage",
    )(table, v, p, q)


def merge_kernel(blk, rows, picks, dense_ref, *refs):
    lists, outs = refs[:-2], refs[-2:]
    width = dense_ref.shape[1]
    for half, out in enumerate(outs):
        for c in range(0, width, LANES):
            part = slice(c, c + LANES)
            items = []
            for ref, numbers in zip(lists, picks):
                for top in (number * (2 * CAP * rows + 8) for number in numbers):
                    for n in range(half * CAP, half * CAP + CAP):
                        at, slot = top + n * rows, top + 2 * CAP * rows + n
                        items.append((ref[slot:slot + 1, part], ref[at:at + rows, part]))
            for b in range(blk):
                at = (half * blk + b) * rows
                total = dense_ref[at:at + rows, part]
                for slot, value in items:
                    total = total + jnp.where(slot == float(b), value, 0.0)
                out[b * rows:(b + 1) * rows, part] = total


def merge(blk, rows, dense, *lists):
    width = dense.shape[1]
    return list(pl.pallas_call(
        functools.partial(merge_kernel, blk, rows, [numbers for _, numbers in lists]),
        out_shape=[jax.ShapeDtypeStruct((blk * rows, width), jnp.float32)] * 2,
        compiler_params=pltpu.CompilerParams(vmem_limit_bytes=6 * MIB),
        cost_estimate=pl.CostEstimate(flops=1000000, bytes_accessed=1000000, transcendentals=0),
        name="merge",
    )(dense, *(ref for ref, _ in lists)))


def edges_kernel(adj0_ref, coef0_ref, adj1_ref, coef1_ref, first_ref, last_ref):
    first_ref[0] = coef0_ref[0] * adj0_ref[0]
    last_ref[0] = coef1_ref[0] * adj1_ref[0]


def edges(adj, coef):
    lev, fields, blk, cols = adj.shape
    shape = (1, fields, blk, cols)
    return pl.pallas_call(
        edges_kernel,
        grid=(1,),
        in_specs=[
            pl.BlockSpec(shape, lambda i: (0, 0, 0, 0)),
            pl.BlockSpec((1, 1, blk, cols), lambda i: (0, 0, 0, 0)),
            pl.BlockSpec(shape, lambda i: (lev - 1, 0, 0, 0)),
            pl.BlockSpec((1, 1, blk, cols), lambda i: (2, lev - 1, 0, 0)),
        ],
        out_specs=[pl.BlockSpec(shape, lambda i: (0, 0, 0, 0))] * 2,
        out_shape=[jax.ShapeDtypeStruct(shape, jnp.float32)] * 2,
        compiler_params=pltpu.CompilerParams(vmem_limit_bytes=60 * MIB),
        name="edges",
    )(adj, coef, adj, coef)


def vertical_kernel(adj_ref, coef_ref, after_ref, before_ref, v_ref):
    lev, fields, blk, cols = adj_ref.shape
    for c in range(0, cols, LANES):
        part = slice(c, c + LANES)
        levels = []
        for m in range(lev):
            low = after_ref[0, :, :, part] if m == lev - 1 else coef_ref[0, m + 1, :, part] * adj_ref[m + 1, :, :, part]
            high = before_ref[0, :, :, part] if m == 0 else coef_ref[2, m - 1, :, part] * adj_ref[m - 1, :, :, part]
            levels.append(low + coef_ref[1, m, :, part] * adj_ref[m, :, :, part] + high)
        whole = jnp.concatenate(levels, 0)
        v_ref[:, :, part] = jnp.swapaxes(whole, 0, 1).astype(jnp.bfloat16)


def vertical(adj, coef, after, before):
    lev, fields, blk, cols = adj.shape
    return pl.pallas_call(
        vertical_kernel,
        out_shape=jax.ShapeDtypeStruct((blk, lev * fields, cols), jnp.bfloat16),
        compiler_params=pltpu.CompilerParams(vmem_limit_bytes=4 * MIB),
        cost_estimate=pl.CostEstimate(flops=1000000, bytes_accessed=1000000, transcendentals=0),
        name="vertical",
    )(adj, coef, after, before)


def shards(adj_arrival, vert_coef, stencil_weight, stencil_cols, dep_owner, dep_slot):
    lev_dev, fields, blk, cols = adj_arrival.shape
    tiles, levels = lax.axis_size("tile"), lax.axis_size("lev")
    deps, points = stencil_weight.shape[1:3]
    items, rows = blk * deps, lev_dev * fields
    chips = tiles // 2
    far = chips // 2

    first, last = edges(adj_arrival, vert_coef)
    after = lax.ppermute(first, "lev", [(i + 1, i) for i in range(levels - 1)])
    before = lax.ppermute(last, "lev", [(i, i + 1) for i in range(levels - 1)])

    p, q, table = placed(
        chips,
        dep_owner,
        dep_slot,
        stencil_weight.reshape(items, points, cols),
        stencil_cols.reshape(items, points, cols),
    )

    v = vertical(adj_arrival, vert_coef, after, before)

    sibling = [(t, t ^ 1) for t in range(tiles)]
    ring = [(t, (t + 2 * (1 - 2 * (t % 2))) % tiles) for t in range(tiles)]
    quad = 2 * CAP

    def made(table, *groups):
        return stage(groups, deps, table, v, p, q)

    def behind(table, value):
        return lax.optimization_barrier((table, value))

    def onward(values, pairs):
        return [lax.ppermute(value, "tile", pairs) for value in values]

    def own_at(h):
        return quad + (far - 1 - h) * 2 * quad

    def other_at(h):
        return own_at(h) + quad

    (listed,) = made(table, ((0,), True))
    table, listed = behind(table, listed)
    (farthest,) = onward([listed], ring)
    near = far - 2
    own, others = made(table, ((own_at(far - 1),), True), ((other_at(far - 1), other_at(near)), True))
    others, farthest = lax.optimization_barrier((others, farthest))
    (given,) = onward([others], sibling)
    table, given = behind(table, given)
    (arrived,) = onward([jnp.concatenate([own, farthest, given[:own.shape[0]]], 0)], ring)

    totals, waiting = None, {near: (given, (1,))}

    def exchanged(table, distances, *others):
        (listed,) = made(table, (tuple(other_at(d) for d in distances), True))
        table, listed, *others = lax.optimization_barrier((table, listed, *others))
        (given,) = onward([listed], sibling)
        waiting.update({d: (given, (number,)) for number, d in enumerate(distances)})
        return table, *others

    for h in range(near, 0, -1):
        (own,) = made(table, ((own_at(h),), False))
        if totals is None:
            table, own = behind(table, own)
            table, own = exchanged(table, range(near - 1, 0, -1), own)
            totals = merge(blk, rows, own, waiting[h], (arrived, (0, 1, 2)))
        else:
            mine = lax.optimization_barrier(merge(blk, rows, own, waiting[h]))
            totals = [total + here for total, here in zip(onward(totals, ring), mine)]
        table, totals[0] = behind(table, totals[0])
    sums = onward(totals, ring)
    (here,) = made(table, ((own_at(0),), False))
    (swapped,) = onward([sums[0] + here[:blk * rows]], sibling)
    result = sums[1] + here[blk * rows:] + swapped
    result = jnp.transpose(result.reshape(blk, rows, cols), (1, 0, 2))
    return result.reshape(lev_dev, fields, blk, cols)


def solution(mesh):
    in_specs = (
        P("lev", None, "tile", None),
        P(None, "lev", "tile", None),
        P("tile", None, None, None),
        P("tile", None, None, None),
        P("tile", None),
        P("tile", None),
    )
    out_specs = P("lev", None, "tile", None)
    return jax.shard_map(shards, mesh=mesh, in_specs=in_specs, out_specs=out_specs, check_vma=False)
```

```python
import functools

import jax
import jax.numpy as jnp
from jax import lax
from jax.experimental import pallas as pl
from jax.experimental.pallas import tpu as pltpu
from jax.sharding import PartitionSpec as P

WIN = 32
SPAN = 96
LANES = 128
TILE = 16
CAP = 2
MIB = 1024 * 1024


def stage_sizes(far):
    return [2 * CAP] + [4 * CAP] * (far - 1) + [2 * CAP]


def fill_table(chips, pair_ref, table, count):
    deps, blk = pair_ref.shape[1:]
    far = chips // 2
    tile = lax.axis_index("tile")
    chip, core = lax.div(tile, 2), lax.rem(tile, 2)
    ahead = 1 - 2 * core
    entries = sum(stage_sizes(far))

    def clear(n, _):
        table[0, n] = jnp.int32(-1)
        table[1, n] = jnp.int32(0)
        return 0

    lax.fori_loop(0, entries, clear, 0)

    def reset(n, _):
        count[n] = jnp.int32(0)
        return 0

    lax.fori_loop(0, 2 * chips, reset, 0)

    def enter(n, _):
        row, k = lax.div(n, deps), lax.rem(n, deps)
        owner = pair_ref[0, k, row]
        turn = count[owner]
        count[owner] = turn + 1
        away = lax.rem(ahead * (lax.div(owner, 2) - chip) + chips, chips)
        back = away > far
        distance = jnp.where(back, chips - away, away)
        own = (lax.rem(owner, 2) == core).astype(jnp.int32)
        half = jnp.where(back, 1 - own, own)
        start = jnp.where(
            away == 0,
            entries - 2 * CAP,
            jnp.where(away == far, 0, 2 * CAP + (far - 1 - distance) * 4 * CAP + jnp.where(back, 2 * CAP, 0)),
        )
        at = start + half * CAP + turn
        table[0, at] = n
        table[1, at] = pair_ref[1, k, row]
        return 0

    lax.fori_loop(0, blk * deps, enter, 0)


def table_kernel(chips, pair_ref, table, count):
    fill_table(chips, pair_ref, table, count)


def item_table(chips, dep_owner, dep_slot):
    entries = sum(stage_sizes(chips // 2))
    smem = pl.BlockSpec(memory_space=pltpu.SMEM)
    return pl.pallas_call(
        functools.partial(table_kernel, chips),
        in_specs=[smem],
        out_specs=smem,
        out_shape=jax.ShapeDtypeStruct((2, entries), jnp.int32),
        scratch_shapes=[pltpu.SMEM((2 * chips,), jnp.int32)],
        compiler_params=pltpu.CompilerParams(vmem_limit_bytes=MIB),
        cost_estimate=pl.CostEstimate(flops=1000000000, bytes_accessed=1000, transcendentals=0),
        name="table",
    )(jnp.stack([dep_owner.T, dep_slot.T]))


def place_item(w, d, x_sc, w_sc, p_sc):
    points, cols = d.shape
    rel = ((d - d[0:1] + cols // 2) & (cols - 1)) - cols // 2
    low = jnp.min(rel, axis=0, keepdims=True)
    base = (d[0:1] + low) & (cols - 1)
    x_sc[...] = (rel - low + (base & (WIN - 1))).astype(jnp.float32)
    w_sc[...] = w.astype(jnp.float32)
    first = lax.broadcasted_iota(jnp.int32, (TILE, LANES), 0)
    places = [(first + i).astype(jnp.float32).astype(jnp.bfloat16) for i in range(0, SPAN, TILE)]
    for t in range(cols // LANES):
        part = slice(t * LANES, (t + 1) * LANES)
        acc = [jnp.zeros((TILE, LANES), jnp.bfloat16)] * len(places)
        for s in range(points):
            x = jnp.broadcast_to(x_sc[s:s + 1, part], (TILE, LANES)).astype(jnp.bfloat16)
            value = jnp.broadcast_to(w_sc[s:s + 1, part], (TILE, LANES)).astype(jnp.bfloat16)
            acc = [jnp.where(place == x, value, total) for place, total in zip(places, acc)]
        for i, total in enumerate(acc):
            p_sc[i * TILE:(i + 1) * TILE, part] = total
    return base // WIN


def item_contribution(v, q, p_sc, v_sc):
    rows, cols = v.shape
    window = jnp.broadcast_to(q.astype(jnp.float32), (rows, cols)).astype(jnp.bfloat16)
    for i in range(cols // WIN):
        v_sc[i * rows:(i + 1) * rows, :] = jnp.where(window == jnp.bfloat16(i), v, jnp.bfloat16(0))
    u = lax.dot_general(
        v_sc[...], p_sc[...], (((1,), (1,)), ((), ())), preferred_element_type=jnp.float32
    )
    u = jnp.concatenate([u, jnp.zeros((u.shape[0], LANES - SPAN), jnp.float32)], 1)
    lane = lax.broadcasted_iota(jnp.int32, (rows, LANES), 1)
    kept, passed = [], []
    for t in range(cols // LANES):
        u0, u1, u2, u3 = (u[(4 * t + j) * rows:(4 * t + j + 1) * rows] for j in range(4))
        kept.append(u0 + pltpu.roll(u1, WIN, 1))
        passed.append(pltpu.roll(u2, 2 * WIN, 1) + pltpu.roll(u3, 3 * WIN, 1))
    return [
        kept[t] + jnp.where(lane >= LANES // 2, passed[t], passed[t - 1]) for t in range(len(kept))
    ]


def stage_kernel(groups, deps, rows, table, v_ref, w_ref, cols_ref, *rest):
    *outs, v_sc, x_sc, w_sc, p_sc = rest
    cols = v_ref.shape[-1]
    blk = v_ref.shape[0]
    for (firsts, listed), out in zip(groups, outs):
        out[...] = jnp.zeros_like(out)
        for number, first in enumerate(firsts):
            top = number * (2 * CAP * rows + 8)
            if listed:
                ids = lax.broadcasted_iota(jnp.int32, (8, cols), 0)
                slots = jnp.zeros((8, cols), jnp.int32)
                for n in range(2 * CAP):
                    slots = jnp.where(ids == n, table[1, first + n], slots)
                out[top + 2 * CAP * rows:top + 2 * CAP * rows + 8, :] = slots.astype(jnp.float32)

            def one(n, _):
                index = table[0, first + n]

                @pl.when(index >= 0)
                def _():
                    q = place_item(w_ref[index], cols_ref[index], x_sc, w_sc, p_sc)
                    parts = item_contribution(v_ref[lax.div(index, deps)], q, p_sc, v_sc)
                    if listed:
                        at = pl.multiple_of(top + n * rows, 8)
                    else:
                        at = pl.multiple_of((lax.div(n, CAP) * blk + table[1, first + n]) * rows, rows)
                    for t, part in enumerate(parts):
                        where = (pl.ds(at, rows), slice(t * LANES, (t + 1) * LANES))
                        out[where] = out[where] + part

                return 0

            lax.fori_loop(0, 2 * CAP, one, 0)


def stage(groups, deps, table, v, weight, places):
    blk, rows, cols = v.shape
    heights = [len(firsts) * (2 * CAP * rows + 8) if listed else 2 * blk * rows for firsts, listed in groups]
    vmem = pl.BlockSpec(memory_space=pltpu.VMEM)
    return pl.pallas_call(
        functools.partial(stage_kernel, groups, deps, rows),
        in_specs=[pl.BlockSpec(memory_space=pltpu.SMEM), vmem, vmem, vmem],
        out_specs=[vmem] * len(groups),
        out_shape=[jax.ShapeDtypeStruct((height, cols), jnp.float32) for height in heights],
        scratch_shapes=[
            pltpu.VMEM((cols // WIN * rows, cols), jnp.bfloat16),
            pltpu.VMEM(weight.shape[1:], jnp.float32),
            pltpu.VMEM(weight.shape[1:], jnp.float32),
            pltpu.VMEM((SPAN, cols), jnp.bfloat16),
        ],
        compiler_params=pltpu.CompilerParams(vmem_limit_bytes=10 * MIB),
        cost_estimate=pl.CostEstimate(
            flops=len(groups) * 200000000, bytes_accessed=500000, transcendentals=0
        ),
        name="stage",
    )(table, v, weight, places)


def merge_kernel(blk, rows, picks, dense_ref, *refs):
    lists, outs = refs[:-2], refs[-2:]
    width = dense_ref.shape[1]
    for half, out in enumerate(outs):
        for c in range(0, width, LANES):
            part = slice(c, c + LANES)
            items = []
            for ref, numbers in zip(lists, picks):
                for top in (number * (2 * CAP * rows + 8) for number in numbers):
                    for n in range(half * CAP, half * CAP + CAP):
                        at, slot = top + n * rows, top + 2 * CAP * rows + n
                        items.append((ref[slot:slot + 1, part], ref[at:at + rows, part]))
            for b in range(blk):
                at = (half * blk + b) * rows
                total = dense_ref[at:at + rows, part]
                for slot, value in items:
                    total = total + jnp.where(slot == float(b), value, 0.0)
                out[b * rows:(b + 1) * rows, part] = total


def merge(blk, rows, dense, *lists):
    width = dense.shape[1]
    return list(pl.pallas_call(
        functools.partial(merge_kernel, blk, rows, [numbers for _, numbers in lists]),
        out_shape=[jax.ShapeDtypeStruct((blk * rows, width), jnp.float32)] * 2,
        compiler_params=pltpu.CompilerParams(vmem_limit_bytes=6 * MIB),
        cost_estimate=pl.CostEstimate(flops=1000000, bytes_accessed=1000000, transcendentals=0),
        name="merge",
    )(dense, *(ref for ref, _ in lists)))


def edges_kernel(adj0_ref, coef0_ref, adj1_ref, coef1_ref, first_ref, last_ref):
    first_ref[0] = coef0_ref[0] * adj0_ref[0]
    last_ref[0] = coef1_ref[0] * adj1_ref[0]


def edges(adj, coef):
    lev, fields, blk, cols = adj.shape
    shape = (1, fields, blk, cols)
    return pl.pallas_call(
        edges_kernel,
        grid=(1,),
        in_specs=[
            pl.BlockSpec(shape, lambda i: (0, 0, 0, 0)),
            pl.BlockSpec((1, 1, blk, cols), lambda i: (0, 0, 0, 0)),
            pl.BlockSpec(shape, lambda i: (lev - 1, 0, 0, 0)),
            pl.BlockSpec((1, 1, blk, cols), lambda i: (2, lev - 1, 0, 0)),
        ],
        out_specs=[pl.BlockSpec(shape, lambda i: (0, 0, 0, 0))] * 2,
        out_shape=[jax.ShapeDtypeStruct(shape, jnp.float32)] * 2,
        compiler_params=pltpu.CompilerParams(vmem_limit_bytes=60 * MIB),
        name="edges",
    )(adj, coef, adj, coef)


def vertical_kernel(adj_ref, coef_ref, after_ref, before_ref, v_ref):
    lev, fields, blk, cols = adj_ref.shape
    for c in range(0, cols, LANES):
        part = slice(c, c + LANES)
        levels = []
        for m in range(lev):
            low = after_ref[0, :, :, part] if m == lev - 1 else coef_ref[0, m + 1, :, part] * adj_ref[m + 1, :, :, part]
            high = before_ref[0, :, :, part] if m == 0 else coef_ref[2, m - 1, :, part] * adj_ref[m - 1, :, :, part]
            levels.append(low + coef_ref[1, m, :, part] * adj_ref[m, :, :, part] + high)
        whole = jnp.concatenate(levels, 0)
        v_ref[:, :, part] = jnp.swapaxes(whole, 0, 1).astype(jnp.bfloat16)


def vertical(adj, coef, after, before):
    lev, fields, blk, cols = adj.shape
    return pl.pallas_call(
        vertical_kernel,
        out_shape=jax.ShapeDtypeStruct((blk, lev * fields, cols), jnp.bfloat16),
        compiler_params=pltpu.CompilerParams(vmem_limit_bytes=4 * MIB),
        cost_estimate=pl.CostEstimate(flops=1000000, bytes_accessed=1000000, transcendentals=0),
        name="vertical",
    )(adj, coef, after, before)


def shards(adj_arrival, vert_coef, stencil_weight, stencil_cols, dep_owner, dep_slot):
    lev_dev, fields, blk, cols = adj_arrival.shape
    tiles, levels = lax.axis_size("tile"), lax.axis_size("lev")
    deps, points = stencil_weight.shape[1:3]
    items, rows = blk * deps, lev_dev * fields
    chips = tiles // 2
    far = chips // 2

    first, last = edges(adj_arrival, vert_coef)
    after = lax.ppermute(first, "lev", [(i + 1, i) for i in range(levels - 1)])
    before = lax.ppermute(last, "lev", [(i, i + 1) for i in range(levels - 1)])

    table = item_table(chips, dep_owner, dep_slot)
    weight = stencil_weight.reshape(items, points, cols)
    places = stencil_cols.reshape(items, points, cols)
    v = vertical(adj_arrival, vert_coef, after, before)

    sibling = [(t, t ^ 1) for t in range(tiles)]
    ring = [(t, (t + 2 * (1 - 2 * (t % 2))) % tiles) for t in range(tiles)]
    quad = 2 * CAP

    def made(table, *groups):
        return stage(groups, deps, table, v, weight, places)

    def behind(table, value):
        return lax.optimization_barrier((table, value))

    def onward(values, pairs):
        return [lax.ppermute(value, "tile", pairs) for value in values]

    def own_at(h):
        return quad + (far - 1 - h) * 2 * quad

    def other_at(h):
        return own_at(h) + quad

    (listed,) = made(table, ((0,), True))
    table, listed = behind(table, listed)
    (farthest,) = onward([listed], ring)
    near = far - 2
    own, others = made(table, ((own_at(far - 1),), True), ((other_at(far - 1), other_at(near)), True))
    others, farthest = lax.optimization_barrier((others, farthest))
    (given,) = onward([others], sibling)
    table, given = behind(table, given)
    (arrived,) = onward([jnp.concatenate([own, farthest, given[:own.shape[0]]], 0)], ring)

    totals, waiting = None, {near: (given, (1,))}

    def exchanged(table, distances, *others):
        (listed,) = made(table, (tuple(other_at(d) for d in distances), True))
        table, listed, *others = lax.optimization_barrier((table, listed, *others))
        (given,) = onward([listed], sibling)
        waiting.update({d: (given, (number,)) for number, d in enumerate(distances)})
        return table, *others

    for h in range(near, 0, -1):
        (own,) = made(table, ((own_at(h),), False))
        if totals is None:
            table, own = behind(table, own)
            table, own = exchanged(table, range(near - 1, 0, -1), own)
            totals = merge(blk, rows, own, waiting[h], (arrived, (0, 1, 2)))
        else:
            mine = lax.optimization_barrier(merge(blk, rows, own, waiting[h]))
            totals = [total + here for total, here in zip(onward(totals, ring), mine)]
        table, totals[0] = behind(table, totals[0])
    sums = onward(totals, ring)
    (here,) = made(table, ((own_at(0),), False))
    (swapped,) = onward([sums[0] + here[:blk * rows]], sibling)
    result = sums[1] + here[blk * rows:] + swapped
    result = jnp.transpose(result.reshape(blk, rows, cols), (1, 0, 2))
    return result.reshape(lev_dev, fields, blk, cols)


def solution(mesh):
    in_specs = (
        P("lev", None, "tile", None),
        P(None, "lev", "tile", None),
        P("tile", None, None, None),
        P("tile", None, None, None),
        P("tile", None),
        P("tile", None),
    )
    out_specs = P("lev", None, "tile", None)
    return jax.shard_map(shards, mesh=mesh, in_specs=in_specs, out_specs=out_specs, check_vma=False)
```

```python
import functools

import jax
import jax.numpy as jnp
from jax import lax
from jax.experimental import pallas as pl
from jax.experimental.pallas import tpu as pltpu
from jax.sharding import PartitionSpec as P

WIN = 32
SPAN = 96
LANES = 128
TILE = 16
CAP = 2
MIB = 1024 * 1024


def stage_sizes(far):
    return [2 * CAP] + [4 * CAP] * (far - 1) + [2 * CAP]


def fill_table(chips, pair_ref, table, count):
    deps, blk = pair_ref.shape[1:]
    far = chips // 2
    tile = lax.axis_index("tile")
    chip, core = lax.div(tile, 2), lax.rem(tile, 2)
    ahead = 1 - 2 * core
    entries = sum(stage_sizes(far))

    for n in range(entries):
        table[0, n] = jnp.int32(-1)
        table[1, n] = jnp.int32(0)
    for n in range(2 * chips):
        count[n] = jnp.int32(0)

    def enter(n, _):
        row, k = lax.div(n, deps), lax.rem(n, deps)
        owner = pair_ref[0, k, row]
        turn = count[owner]
        count[owner] = turn + 1
        away = lax.rem(ahead * (lax.div(owner, 2) - chip) + chips, chips)
        back = away > far
        distance = jnp.where(back, chips - away, away)
        own = (lax.rem(owner, 2) == core).astype(jnp.int32)
        half = jnp.where(back, 1 - own, own)
        start = jnp.where(
            away == 0,
            entries - 2 * CAP,
            jnp.where(away == far, 0, 2 * CAP + (far - 1 - distance) * 4 * CAP + jnp.where(back, 2 * CAP, 0)),
        )
        at = start + half * CAP + turn
        table[0, at] = n
        table[1, at] = pair_ref[1, k, row]
        return 0

    lax.fori_loop(0, blk * deps, enter, 0)


def table_kernel(chips, pair_ref, table, count):
    fill_table(chips, pair_ref, table, count)


def item_table(chips, dep_owner, dep_slot):
    entries = sum(stage_sizes(chips // 2))
    smem = pl.BlockSpec(memory_space=pltpu.SMEM)
    return pl.pallas_call(
        functools.partial(table_kernel, chips),
        in_specs=[smem],
        out_specs=smem,
        out_shape=jax.ShapeDtypeStruct((2, entries), jnp.int32),
        scratch_shapes=[pltpu.SMEM((2 * chips,), jnp.int32)],
        compiler_params=pltpu.CompilerParams(vmem_limit_bytes=MIB),
        cost_estimate=pl.CostEstimate(flops=1000000000, bytes_accessed=1000, transcendentals=0),
        name="table",
    )(jnp.stack([dep_owner.T, dep_slot.T]))


def place_item(w, d, x_sc, w_sc, p_sc):
    points, cols = d.shape
    rel = ((d - d[0:1] + cols // 2) & (cols - 1)) - cols // 2
    low = jnp.min(rel, axis=0, keepdims=True)
    base = (d[0:1] + low) & (cols - 1)
    x_sc[...] = (rel - low + (base & (WIN - 1))).astype(jnp.float32)
    w_sc[...] = w.astype(jnp.float32)
    first = lax.broadcasted_iota(jnp.int32, (TILE, LANES), 0)
    places = [(first + i).astype(jnp.float32).astype(jnp.bfloat16) for i in range(0, SPAN, TILE)]
    for t in range(cols // LANES):
        part = slice(t * LANES, (t + 1) * LANES)
        acc = [jnp.zeros((TILE, LANES), jnp.bfloat16)] * len(places)
        for s in range(points):
            x = jnp.broadcast_to(x_sc[s:s + 1, part], (TILE, LANES)).astype(jnp.bfloat16)
            value = jnp.broadcast_to(w_sc[s:s + 1, part], (TILE, LANES)).astype(jnp.bfloat16)
            acc = [jnp.where(place == x, value, total) for place, total in zip(places, acc)]
        for i, total in enumerate(acc):
            p_sc[i * TILE:(i + 1) * TILE, part] = total
    return base // WIN


def place_kernel(slots, table, w_ref, cols_ref, p_ref, q_ref, x_sc, w_sc):
    def one(n, _):
        index = table[0, n]

        @pl.when(index >= 0)
        def _():
            q_ref[n, 0:1, :] = place_item(w_ref[index], cols_ref[index], x_sc, w_sc, p_ref.at[n])

        return 0

    lax.fori_loop(0, slots, one, 0)


def placed(slots, table, weight, places):
    points, cols = weight.shape[1:]
    vmem = pl.BlockSpec(memory_space=pltpu.VMEM)
    return pl.pallas_call(
        functools.partial(place_kernel, slots),
        in_specs=[pl.BlockSpec(memory_space=pltpu.SMEM), vmem, vmem],
        out_specs=[vmem, vmem],
        out_shape=[
            jax.ShapeDtypeStruct((slots, SPAN, cols), jnp.bfloat16),
            jax.ShapeDtypeStruct((slots, 8, cols), jnp.int32),
        ],
        scratch_shapes=[
            pltpu.VMEM((points, cols), jnp.float32),
            pltpu.VMEM((points, cols), jnp.float32),
        ],
        compiler_params=pltpu.CompilerParams(vmem_limit_bytes=8 * MIB),
        cost_estimate=pl.CostEstimate(flops=3000000000, bytes_accessed=1000, transcendentals=0),
        name="place",
    )(table, weight, places)


def item_contribution(v, q, p_ref, v_sc):
    rows, cols = v.shape
    window = jnp.broadcast_to(q.astype(jnp.float32), (rows, cols)).astype(jnp.bfloat16)
    for i in range(cols // WIN):
        v_sc[i * rows:(i + 1) * rows, :] = jnp.where(window == jnp.bfloat16(i), v, jnp.bfloat16(0))
    u = lax.dot_general(
        v_sc[...], p_ref[...], (((1,), (1,)), ((), ())), preferred_element_type=jnp.float32
    )
    u = jnp.concatenate([u, jnp.zeros((u.shape[0], LANES - SPAN), jnp.float32)], 1)
    lane = lax.broadcasted_iota(jnp.int32, (rows, LANES), 1)
    kept, passed = [], []
    for t in range(cols // LANES):
        u0, u1, u2, u3 = (u[(4 * t + j) * rows:(4 * t + j + 1) * rows] for j in range(4))
        kept.append(u0 + pltpu.roll(u1, WIN, 1))
        passed.append(pltpu.roll(u2, 2 * WIN, 1) + pltpu.roll(u3, 3 * WIN, 1))
    return [
        kept[t] + jnp.where(lane >= LANES // 2, passed[t], passed[t - 1]) for t in range(len(kept))
    ]


def stage_kernel(groups, deps, rows, ready, table, v_ref, w_ref, cols_ref, *rest):
    outs, v_sc, places = rest[:len(groups)], rest[len(groups)], rest[len(groups) + 1:]
    cols = v_ref.shape[-1]
    blk = v_ref.shape[0]
    for (firsts, listed), out in zip(groups, outs):
        out[...] = jnp.zeros_like(out)
        for number, first in enumerate(firsts):
            top = number * (2 * CAP * rows + 8)
            if listed:
                ids = lax.broadcasted_iota(jnp.int32, (8, cols), 0)
                slots = jnp.zeros((8, cols), jnp.int32)
                for n in range(2 * CAP):
                    slots = jnp.where(ids == n, table[1, first + n], slots)
                out[top + 2 * CAP * rows:top + 2 * CAP * rows + 8, :] = slots.astype(jnp.float32)

            def one(n, _):
                index = table[0, first + n]

                @pl.when(index >= 0)
                def _():
                    if ready:
                        p, q = w_ref.at[first + n], cols_ref[first + n, 0:1, :]
                    else:
                        x_sc, w_sc, p = places
                        q = place_item(w_ref[index], cols_ref[index], x_sc, w_sc, p)
                    parts = item_contribution(v_ref[lax.div(index, deps)], q, p, v_sc)
                    if listed:
                        at = pl.multiple_of(top + n * rows, 8)
                    else:
                        at = pl.multiple_of((lax.div(n, CAP) * blk + table[1, first + n]) * rows, rows)
                    for t, part in enumerate(parts):
                        where = (pl.ds(at, rows), slice(t * LANES, (t + 1) * LANES))
                        out[where] = out[where] + part

                return 0

            lax.fori_loop(0, 2 * CAP, one, 0)


def stage(groups, deps, ready, table, v, weight, places):
    blk, rows, cols = v.shape
    heights = [len(firsts) * (2 * CAP * rows + 8) if listed else 2 * blk * rows for firsts, listed in groups]
    vmem = pl.BlockSpec(memory_space=pltpu.VMEM)
    return pl.pallas_call(
        functools.partial(stage_kernel, groups, deps, rows, ready),
        in_specs=[pl.BlockSpec(memory_space=pltpu.SMEM), vmem, vmem, vmem],
        out_specs=[vmem] * len(groups),
        out_shape=[jax.ShapeDtypeStruct((height, cols), jnp.float32) for height in heights],
        scratch_shapes=[
            pltpu.VMEM((cols // WIN * rows, cols), jnp.bfloat16),
        ] + ([] if ready else [
            pltpu.VMEM(weight.shape[1:], jnp.float32),
            pltpu.VMEM(weight.shape[1:], jnp.float32),
            pltpu.VMEM((SPAN, cols), jnp.bfloat16),
        ]),
        compiler_params=pltpu.CompilerParams(vmem_limit_bytes=10 * MIB),
        cost_estimate=pl.CostEstimate(
            flops=len(groups) * 200000000, bytes_accessed=500000, transcendentals=0
        ),
        name="stage",
    )(table, v, weight, places)


def merge_kernel(blk, rows, picks, dense_ref, *refs):
    lists, outs = refs[:-2], refs[-2:]
    width = dense_ref.shape[1]
    for half, out in enumerate(outs):
        for c in range(0, width, LANES):
            part = slice(c, c + LANES)
            items = []
            for ref, numbers in zip(lists, picks):
                for top in (number * (2 * CAP * rows + 8) for number in numbers):
                    for n in range(half * CAP, half * CAP + CAP):
                        at, slot = top + n * rows, top + 2 * CAP * rows + n
                        items.append((ref[slot:slot + 1, part], ref[at:at + rows, part]))
            for b in range(blk):
                at = (half * blk + b) * rows
                total = dense_ref[at:at + rows, part]
                for slot, value in items:
                    total = total + jnp.where(slot == float(b), value, 0.0)
                out[b * rows:(b + 1) * rows, part] = total


def merge(blk, rows, dense, *lists):
    width = dense.shape[1]
    return list(pl.pallas_call(
        functools.partial(merge_kernel, blk, rows, [numbers for _, numbers in lists]),
        out_shape=[jax.ShapeDtypeStruct((blk * rows, width), jnp.float32)] * 2,
        compiler_params=pltpu.CompilerParams(vmem_limit_bytes=6 * MIB),
        cost_estimate=pl.CostEstimate(flops=1000000, bytes_accessed=1000000, transcendentals=0),
        name="merge",
    )(dense, *(ref for ref, _ in lists)))


def edges_kernel(adj0_ref, coef0_ref, adj1_ref, coef1_ref, first_ref, last_ref):
    first_ref[0] = coef0_ref[0] * adj0_ref[0]
    last_ref[0] = coef1_ref[0] * adj1_ref[0]


def edges(adj, coef):
    lev, fields, blk, cols = adj.shape
    shape = (1, fields, blk, cols)
    return pl.pallas_call(
        edges_kernel,
        grid=(1,),
        in_specs=[
            pl.BlockSpec(shape, lambda i: (0, 0, 0, 0)),
            pl.BlockSpec((1, 1, blk, cols), lambda i: (0, 0, 0, 0)),
            pl.BlockSpec(shape, lambda i: (lev - 1, 0, 0, 0)),
            pl.BlockSpec((1, 1, blk, cols), lambda i: (2, lev - 1, 0, 0)),
        ],
        out_specs=[pl.BlockSpec(shape, lambda i: (0, 0, 0, 0))] * 2,
        out_shape=[jax.ShapeDtypeStruct(shape, jnp.float32)] * 2,
        compiler_params=pltpu.CompilerParams(vmem_limit_bytes=60 * MIB),
        name="edges",
    )(adj, coef, adj, coef)


def vertical_kernel(adj_ref, coef_ref, after_ref, before_ref, v_ref):
    lev, fields, blk, cols = adj_ref.shape
    for c in range(0, cols, LANES):
        part = slice(c, c + LANES)
        levels = []
        for m in range(lev):
            low = after_ref[0, :, :, part] if m == lev - 1 else coef_ref[0, m + 1, :, part] * adj_ref[m + 1, :, :, part]
            high = before_ref[0, :, :, part] if m == 0 else coef_ref[2, m - 1, :, part] * adj_ref[m - 1, :, :, part]
            levels.append(low + coef_ref[1, m, :, part] * adj_ref[m, :, :, part] + high)
        whole = jnp.concatenate(levels, 0)
        v_ref[:, :, part] = jnp.swapaxes(whole, 0, 1).astype(jnp.bfloat16)


def vertical(adj, coef, after, before):
    lev, fields, blk, cols = adj.shape
    return pl.pallas_call(
        vertical_kernel,
        out_shape=jax.ShapeDtypeStruct((blk, lev * fields, cols), jnp.bfloat16),
        compiler_params=pltpu.CompilerParams(vmem_limit_bytes=4 * MIB),
        cost_estimate=pl.CostEstimate(flops=1000000, bytes_accessed=1000000, transcendentals=0),
        name="vertical",
    )(adj, coef, after, before)


def shards(adj_arrival, vert_coef, stencil_weight, stencil_cols, dep_owner, dep_slot):
    lev_dev, fields, blk, cols = adj_arrival.shape
    tiles, levels = lax.axis_size("tile"), lax.axis_size("lev")
    deps, points = stencil_weight.shape[1:3]
    items, rows = blk * deps, lev_dev * fields
    chips = tiles // 2
    far = chips // 2

    first, last = edges(adj_arrival, vert_coef)
    after = lax.ppermute(first, "lev", [(i + 1, i) for i in range(levels - 1)])
    before = lax.ppermute(last, "lev", [(i, i + 1) for i in range(levels - 1)])

    table = item_table(chips, dep_owner, dep_slot)
    weight = stencil_weight.reshape(items, points, cols)
    places = stencil_cols.reshape(items, points, cols)
    early = 5 * 2 * CAP
    p, q = placed(early, table, weight, places)
    v = vertical(adj_arrival, vert_coef, after, before)

    sibling = [(t, t ^ 1) for t in range(tiles)]
    ring = [(t, (t + 2 * (1 - 2 * (t % 2))) % tiles) for t in range(tiles)]
    quad = 2 * CAP

    def made(table, *groups):
        ready = max(first for firsts, _ in groups for first in firsts) < early
        return stage(groups, deps, ready, table, v, *((p, q) if ready else (weight, places)))

    def behind(table, value):
        return lax.optimization_barrier((table, value))

    def onward(values, pairs):
        return [lax.ppermute(value, "tile", pairs) for value in values]

    def own_at(h):
        return quad + (far - 1 - h) * 2 * quad

    def other_at(h):
        return own_at(h) + quad

    (listed,) = made(table, ((0,), True))
    table, listed = behind(table, listed)
    (farthest,) = onward([listed], ring)
    near = far - 2
    (others,) = made(table, ((other_at(far - 1), other_at(near)), True))
    table, others = behind(table, others)
    (own,) = made(table, ((own_at(far - 1),), True))
    others, farthest = lax.optimization_barrier((others, farthest))
    (given,) = onward([others], sibling)
    table, given = behind(table, given)
    (arrived,) = onward([jnp.concatenate([own, farthest, given[:own.shape[0]]], 0)], ring)

    totals, waiting = None, {near: (given, (1,))}

    def exchanged(table, distances, *others):
        (listed,) = made(table, (tuple(other_at(d) for d in distances), True))
        table, listed, *others = lax.optimization_barrier((table, listed, *others))
        (given,) = onward([listed], sibling)
        waiting.update({d: (given, (number,)) for number, d in enumerate(distances)})
        return table, *others

    for h in range(near, 0, -1):
        (own,) = made(table, ((own_at(h),), False))
        if totals is None:
            table, own = behind(table, own)
            table, own = exchanged(table, range(near - 1, 0, -1), own)
            totals = merge(blk, rows, own, waiting[h], (arrived, (0, 1, 2)))
        else:
            mine = lax.optimization_barrier(merge(blk, rows, own, waiting[h]))
            totals = [total + here for total, here in zip(onward(totals, ring), mine)]
        table, totals[0] = behind(table, totals[0])
    sums = onward(totals, ring)
    (here,) = made(table, ((own_at(0),), False))
    (swapped,) = onward([sums[0] + here[:blk * rows]], sibling)
    result = sums[1] + here[blk * rows:] + swapped
    result = jnp.transpose(result.reshape(blk, rows, cols), (1, 0, 2))
    return result.reshape(lev_dev, fields, blk, cols)


def solution(mesh):
    in_specs = (
        P("lev", None, "tile", None),
        P(None, "lev", "tile", None),
        P("tile", None, None, None),
        P("tile", None, None, None),
        P("tile", None),
        P("tile", None),
    )
    out_specs = P("lev", None, "tile", None)
    return jax.shard_map(shards, mesh=mesh, in_specs=in_specs, out_specs=out_specs, check_vma=False)
```

```python
import functools

import jax
import jax.numpy as jnp
from jax import lax
from jax.experimental import pallas as pl
from jax.experimental.pallas import tpu as pltpu
from jax.sharding import PartitionSpec as P

WIN = 32
SPAN = 96
LANES = 128
TILE = 16
CAP = 2
MIB = 1024 * 1024


def stage_sizes(far):
    return [2 * CAP] + [4 * CAP] * (far - 1) + [2 * CAP]


def fill_table(chips, pair_ref, table, count):
    deps, blk = pair_ref.shape[1:]
    far = chips // 2
    tile = lax.axis_index("tile")
    chip, core = tile >> 1, tile & 1
    ahead = 1 - 2 * core
    entries = sum(stage_sizes(far))

    for n in range(entries):
        table[0, n] = jnp.int32(-1)
        table[1, n] = jnp.int32(0)
    for n in range(2 * chips):
        count[n] = jnp.int32(0)

    for row in range(blk):
        for k in range(deps):
            owner = pair_ref[0, k, row]
            turn = count[owner]
            count[owner] = turn + 1
            away = ahead * ((owner >> 1) - chip)
            away = jnp.where(away < 0, away + chips, away)
            back = away > far
            distance = jnp.where(back, chips - away, away)
            own = jnp.where((owner & 1) == core, 1, 0)
            half = jnp.where(back, 1 - own, own)
            start = jnp.where(
                away == 0,
                entries - 2 * CAP,
                jnp.where(away == far, 0, 2 * CAP + (far - 1 - distance) * 4 * CAP + jnp.where(back, 2 * CAP, 0)),
            )
            at = start + half * CAP + turn
            table[0, at] = jnp.int32(row * deps + k)
            table[1, at] = pair_ref[1, k, row]


def table_kernel(chips, pair_ref, table, count):
    fill_table(chips, pair_ref, table, count)


def item_table(chips, dep_owner, dep_slot):
    entries = sum(stage_sizes(chips // 2))
    smem = pl.BlockSpec(memory_space=pltpu.SMEM)
    return pl.pallas_call(
        functools.partial(table_kernel, chips),
        in_specs=[smem],
        out_specs=smem,
        out_shape=jax.ShapeDtypeStruct((2, entries), jnp.int32),
        scratch_shapes=[pltpu.SMEM((2 * chips,), jnp.int32)],
        compiler_params=pltpu.CompilerParams(vmem_limit_bytes=MIB),
        cost_estimate=pl.CostEstimate(flops=1000000000, bytes_accessed=1000, transcendentals=0),
        name="table",
    )(jnp.stack([dep_owner.T, dep_slot.T]))


def place_item(w, d, x_sc, w_sc, p_sc):
    points, cols = d.shape
    rel = ((d - d[0:1] + cols // 2) & (cols - 1)) - cols // 2
    low = jnp.min(rel, axis=0, keepdims=True)
    base = (d[0:1] + low) & (cols - 1)
    x_sc[...] = (rel - low + (base & (WIN - 1))).astype(jnp.float32)
    w_sc[...] = w.astype(jnp.float32)
    first = lax.broadcasted_iota(jnp.int32, (TILE, LANES), 0)
    places = [(first + i).astype(jnp.float32).astype(jnp.bfloat16) for i in range(0, SPAN, TILE)]
    for t in range(cols // LANES):
        part = slice(t * LANES, (t + 1) * LANES)
        acc = [jnp.zeros((TILE, LANES), jnp.bfloat16)] * len(places)
        for s in range(points):
            x = jnp.broadcast_to(x_sc[s:s + 1, part], (TILE, LANES)).astype(jnp.bfloat16)
            value = jnp.broadcast_to(w_sc[s:s + 1, part], (TILE, LANES)).astype(jnp.bfloat16)
            acc = [jnp.where(place == x, value, total) for place, total in zip(places, acc)]
        for i, total in enumerate(acc):
            p_sc[i * TILE:(i + 1) * TILE, part] = total
    return base // WIN


def place_kernel(slots, table, w_ref, cols_ref, p_ref, q_ref, x_sc, w_sc):
    def one(n, _):
        index = table[0, n]

        @pl.when(index >= 0)
        def _():
            q_ref[n, 0:1, :] = place_item(w_ref[index], cols_ref[index], x_sc, w_sc, p_ref.at[n])

        return 0

    lax.fori_loop(0, slots, one, 0)


def placed(slots, table, weight, places):
    points, cols = weight.shape[1:]
    vmem = pl.BlockSpec(memory_space=pltpu.VMEM)
    return pl.pallas_call(
        functools.partial(place_kernel, slots),
        in_specs=[pl.BlockSpec(memory_space=pltpu.SMEM), vmem, vmem],
        out_specs=[vmem, vmem],
        out_shape=[
            jax.ShapeDtypeStruct((slots, SPAN, cols), jnp.bfloat16),
            jax.ShapeDtypeStruct((slots, 8, cols), jnp.int32),
        ],
        scratch_shapes=[
            pltpu.VMEM((points, cols), jnp.float32),
            pltpu.VMEM((points, cols), jnp.float32),
        ],
        compiler_params=pltpu.CompilerParams(vmem_limit_bytes=8 * MIB),
        cost_estimate=pl.CostEstimate(flops=3000000000, bytes_accessed=1000, transcendentals=0),
        name="place",
    )(table, weight, places)


def item_contribution(v, q, p_ref, v_sc):
    rows, cols = v.shape
    window = jnp.broadcast_to(q.astype(jnp.float32), (rows, cols)).astype(jnp.bfloat16)
    for i in range(cols // WIN):
        v_sc[i * rows:(i + 1) * rows, :] = jnp.where(window == jnp.bfloat16(i), v, jnp.bfloat16(0))
    u = lax.dot_general(
        v_sc[...], p_ref[...], (((1,), (1,)), ((), ())), preferred_element_type=jnp.float32
    )
    u = jnp.concatenate([u, jnp.zeros((u.shape[0], LANES - SPAN), jnp.float32)], 1)
    lane = lax.broadcasted_iota(jnp.int32, (rows, LANES), 1)
    kept, passed = [], []
    for t in range(cols // LANES):
        u0, u1, u2, u3 = (u[(4 * t + j) * rows:(4 * t + j + 1) * rows] for j in range(4))
        kept.append(u0 + pltpu.roll(u1, WIN, 1))
        passed.append(pltpu.roll(u2, 2 * WIN, 1) + pltpu.roll(u3, 3 * WIN, 1))
    return [
        kept[t] + jnp.where(lane >= LANES // 2, passed[t], passed[t - 1]) for t in range(len(kept))
    ]


def stage_kernel(groups, deps, rows, ready, table, v_ref, w_ref, cols_ref, *rest):
    outs, v_sc, places = rest[:len(groups)], rest[len(groups)], rest[len(groups) + 1:]
    cols = v_ref.shape[-1]
    blk = v_ref.shape[0]
    for (firsts, listed), out in zip(groups, outs):
        out[...] = jnp.zeros_like(out)
        for number, first in enumerate(firsts):
            top = number * (2 * CAP * rows + 8)
            if listed:
                ids = lax.broadcasted_iota(jnp.int32, (8, cols), 0)
                slots = jnp.zeros((8, cols), jnp.int32)
                for n in range(2 * CAP):
                    slots = jnp.where(ids == n, table[1, first + n], slots)
                out[top + 2 * CAP * rows:top + 2 * CAP * rows + 8, :] = slots.astype(jnp.float32)

            def one(n, _):
                index = table[0, first + n]

                @pl.when(index >= 0)
                def _():
                    if ready:
                        p, q = w_ref.at[first + n], cols_ref[first + n, 0:1, :]
                    else:
                        x_sc, w_sc, p = places
                        q = place_item(w_ref[index], cols_ref[index], x_sc, w_sc, p)
                    parts = item_contribution(v_ref[lax.div(index, deps)], q, p, v_sc)
                    if listed:
                        at = pl.multiple_of(top + n * rows, 8)
                    else:
                        at = pl.multiple_of((lax.div(n, CAP) * blk + table[1, first + n]) * rows, rows)
                    for t, part in enumerate(parts):
                        where = (pl.ds(at, rows), slice(t * LANES, (t + 1) * LANES))
                        out[where] = out[where] + part

                return 0

            lax.fori_loop(0, 2 * CAP, one, 0)


def stage(groups, deps, ready, table, v, weight, places):
    blk, rows, cols = v.shape
    heights = [len(firsts) * (2 * CAP * rows + 8) if listed else 2 * blk * rows for firsts, listed in groups]
    vmem = pl.BlockSpec(memory_space=pltpu.VMEM)
    return pl.pallas_call(
        functools.partial(stage_kernel, groups, deps, rows, ready),
        in_specs=[pl.BlockSpec(memory_space=pltpu.SMEM), vmem, vmem, vmem],
        out_specs=[vmem] * len(groups),
        out_shape=[jax.ShapeDtypeStruct((height, cols), jnp.float32) for height in heights],
        scratch_shapes=[
            pltpu.VMEM((cols // WIN * rows, cols), jnp.bfloat16),
        ] + ([] if ready else [
            pltpu.VMEM(weight.shape[1:], jnp.float32),
            pltpu.VMEM(weight.shape[1:], jnp.float32),
            pltpu.VMEM((SPAN, cols), jnp.bfloat16),
        ]),
        compiler_params=pltpu.CompilerParams(vmem_limit_bytes=10 * MIB),
        cost_estimate=pl.CostEstimate(
            flops=len(groups) * 200000000, bytes_accessed=500000, transcendentals=0
        ),
        name="stage",
    )(table, v, weight, places)


def merge_kernel(blk, rows, picks, dense_ref, *refs):
    lists, outs = refs[:-2], refs[-2:]
    width = dense_ref.shape[1]
    for half, out in enumerate(outs):
        for c in range(0, width, LANES):
            part = slice(c, c + LANES)
            items = []
            for ref, numbers in zip(lists, picks):
                for top in (number * (2 * CAP * rows + 8) for number in numbers):
                    for n in range(half * CAP, half * CAP + CAP):
                        at, slot = top + n * rows, top + 2 * CAP * rows + n
                        items.append((ref[slot:slot + 1, part], ref[at:at + rows, part]))
            for b in range(blk):
                at = (half * blk + b) * rows
                total = dense_ref[at:at + rows, part]
                for slot, value in items:
                    total = total + jnp.where(slot == float(b), value, 0.0)
                out[b * rows:(b + 1) * rows, part] = total


def merge(blk, rows, dense, *lists):
    width = dense.shape[1]
    return list(pl.pallas_call(
        functools.partial(merge_kernel, blk, rows, [numbers for _, numbers in lists]),
        out_shape=[jax.ShapeDtypeStruct((blk * rows, width), jnp.float32)] * 2,
        compiler_params=pltpu.CompilerParams(vmem_limit_bytes=6 * MIB),
        cost_estimate=pl.CostEstimate(flops=1000000, bytes_accessed=1000000, transcendentals=0),
        name="merge",
    )(dense, *(ref for ref, _ in lists)))


def edges_kernel(adj0_ref, coef0_ref, adj1_ref, coef1_ref, first_ref, last_ref):
    first_ref[0] = coef0_ref[0] * adj0_ref[0]
    last_ref[0] = coef1_ref[0] * adj1_ref[0]


def edges(adj, coef):
    lev, fields, blk, cols = adj.shape
    shape = (1, fields, blk, cols)
    return pl.pallas_call(
        edges_kernel,
        grid=(1,),
        in_specs=[
            pl.BlockSpec(shape, lambda i: (0, 0, 0, 0)),
            pl.BlockSpec((1, 1, blk, cols), lambda i: (0, 0, 0, 0)),
            pl.BlockSpec(shape, lambda i: (lev - 1, 0, 0, 0)),
            pl.BlockSpec((1, 1, blk, cols), lambda i: (2, lev - 1, 0, 0)),
        ],
        out_specs=[pl.BlockSpec(shape, lambda i: (0, 0, 0, 0))] * 2,
        out_shape=[jax.ShapeDtypeStruct(shape, jnp.float32)] * 2,
        compiler_params=pltpu.CompilerParams(vmem_limit_bytes=60 * MIB),
        name="edges",
    )(adj, coef, adj, coef)


def vertical_kernel(adj_ref, coef_ref, after_ref, before_ref, v_ref):
    lev, fields, blk, cols = adj_ref.shape
    for c in range(0, cols, LANES):
        part = slice(c, c + LANES)
        levels = []
        for m in range(lev):
            low = after_ref[0, :, :, part] if m == lev - 1 else coef_ref[0, m + 1, :, part] * adj_ref[m + 1, :, :, part]
            high = before_ref[0, :, :, part] if m == 0 else coef_ref[2, m - 1, :, part] * adj_ref[m - 1, :, :, part]
            levels.append(low + coef_ref[1, m, :, part] * adj_ref[m, :, :, part] + high)
        whole = jnp.concatenate(levels, 0)
        v_ref[:, :, part] = jnp.swapaxes(whole, 0, 1).astype(jnp.bfloat16)


def vertical(adj, coef, after, before):
    lev, fields, blk, cols = adj.shape
    return pl.pallas_call(
        vertical_kernel,
        out_shape=jax.ShapeDtypeStruct((blk, lev * fields, cols), jnp.bfloat16),
        compiler_params=pltpu.CompilerParams(vmem_limit_bytes=4 * MIB),
        cost_estimate=pl.CostEstimate(flops=1000000, bytes_accessed=1000000, transcendentals=0),
        name="vertical",
    )(adj, coef, after, before)


def shards(adj_arrival, vert_coef, stencil_weight, stencil_cols, dep_owner, dep_slot):
    lev_dev, fields, blk, cols = adj_arrival.shape
    tiles, levels = lax.axis_size("tile"), lax.axis_size("lev")
    deps, points = stencil_weight.shape[1:3]
    items, rows = blk * deps, lev_dev * fields
    chips = tiles // 2
    far = chips // 2

    first, last = edges(adj_arrival, vert_coef)
    after = lax.ppermute(first, "lev", [(i + 1, i) for i in range(levels - 1)])
    before = lax.ppermute(last, "lev", [(i, i + 1) for i in range(levels - 1)])

    table = item_table(chips, dep_owner, dep_slot)
    weight = stencil_weight.reshape(items, points, cols)
    places = stencil_cols.reshape(items, points, cols)
    early = 5 * 2 * CAP
    p, q = placed(early, table, weight, places)
    v = vertical(adj_arrival, vert_coef, after, before)

    sibling = [(t, t ^ 1) for t in range(tiles)]
    ring = [(t, (t + 2 * (1 - 2 * (t % 2))) % tiles) for t in range(tiles)]
    quad = 2 * CAP

    def made(table, *groups):
        ready = max(first for firsts, _ in groups for first in firsts) < early
        return stage(groups, deps, ready, table, v, *((p, q) if ready else (weight, places)))

    def behind(table, value):
        return lax.optimization_barrier((table, value))

    def onward(values, pairs):
        return [lax.ppermute(value, "tile", pairs) for value in values]

    def own_at(h):
        return quad + (far - 1 - h) * 2 * quad

    def other_at(h):
        return own_at(h) + quad

    (listed,) = made(table, ((0,), True))
    table, listed = behind(table, listed)
    (farthest,) = onward([listed], ring)
    near = far - 2
    (others,) = made(table, ((other_at(far - 1), other_at(near)), True))
    table, others = behind(table, others)
    (own,) = made(table, ((own_at(far - 1),), True))
    others, farthest = lax.optimization_barrier((others, farthest))
    (given,) = onward([others], sibling)
    table, given = behind(table, given)
    (arrived,) = onward([jnp.concatenate([own, farthest, given[:own.shape[0]]], 0)], ring)

    totals, waiting = None, {near: (given, (1,))}

    def exchanged(table, distances, *others):
        (listed,) = made(table, (tuple(other_at(d) for d in distances), True))
        table, listed, *others = lax.optimization_barrier((table, listed, *others))
        (given,) = onward([listed], sibling)
        waiting.update({d: (given, (number,)) for number, d in enumerate(distances)})
        return table, *others

    for h in range(near, 0, -1):
        (own,) = made(table, ((own_at(h),), False))
        if totals is None:
            table, own = behind(table, own)
            table, own = exchanged(table, range(near - 1, 0, -1), own)
            totals = merge(blk, rows, own, waiting[h], (arrived, (0, 1, 2)))
        else:
            mine = lax.optimization_barrier(merge(blk, rows, own, waiting[h]))
            totals = [total + here for total, here in zip(onward(totals, ring), mine)]
        table, totals[0] = behind(table, totals[0])
    sums = onward(totals, ring)
    (here,) = made(table, ((own_at(0),), False))
    (swapped,) = onward([sums[0] + here[:blk * rows]], sibling)
    result = sums[1] + here[blk * rows:] + swapped
    result = jnp.transpose(result.reshape(blk, rows, cols), (1, 0, 2))
    return result.reshape(lev_dev, fields, blk, cols)


def solution(mesh):
    in_specs = (
        P("lev", None, "tile", None),
        P(None, "lev", "tile", None),
        P("tile", None, None, None),
        P("tile", None, None, None),
        P("tile", None),
        P("tile", None),
    )
    out_specs = P("lev", None, "tile", None)
    return jax.shard_map(shards, mesh=mesh, in_specs=in_specs, out_specs=out_specs, check_vma=False)
```

```python
import functools

import jax
import jax.numpy as jnp
from jax import lax
from jax.experimental import pallas as pl
from jax.experimental.pallas import tpu as pltpu
from jax.sharding import PartitionSpec as P

WIN = 32
SPAN = 96
LANES = 128
TILE = 16
CAP = 2
MIB = 1024 * 1024


def stage_sizes(far):
    return [2 * CAP] + [4 * CAP] * (far - 1) + [2 * CAP]


def fill_table(chips, pair_ref, table, count):
    deps, blk = pair_ref.shape[1:]
    far = chips // 2
    tile = lax.axis_index("tile")
    chip, core = tile >> 1, tile & 1
    ahead = 1 - 2 * core
    entries = sum(stage_sizes(far))

    for n in range(entries):
        table[0, n] = jnp.int32(-1)
        table[1, n] = jnp.int32(0)
    for n in range(2 * chips):
        count[n] = jnp.int32(0)

    for row in range(blk):
        for k in range(deps):
            owner = pair_ref[0, k, row]
            turn = count[owner]
            count[owner] = turn + 1
            away = ahead * ((owner >> 1) - chip)
            away = jnp.where(away < 0, away + chips, away)
            back = away > far
            distance = jnp.where(back, chips - away, away)
            own = jnp.where((owner & 1) == core, 1, 0)
            half = jnp.where(back, 1 - own, own)
            start = jnp.where(
                away == 0,
                entries - 2 * CAP,
                jnp.where(away == far, 0, 2 * CAP + (far - 1 - distance) * 4 * CAP + jnp.where(back, 2 * CAP, 0)),
            )
            at = start + half * CAP + turn
            table[0, at] = jnp.int32(row * deps + k)
            table[1, at] = pair_ref[1, k, row]


def table_kernel(chips, pair_ref, table, count):
    fill_table(chips, pair_ref, table, count)


def item_table(chips, dep_owner, dep_slot):
    entries = sum(stage_sizes(chips // 2))
    smem = pl.BlockSpec(memory_space=pltpu.SMEM)
    return pl.pallas_call(
        functools.partial(table_kernel, chips),
        in_specs=[smem],
        out_specs=smem,
        out_shape=jax.ShapeDtypeStruct((2, entries), jnp.int32),
        scratch_shapes=[pltpu.SMEM((2 * chips,), jnp.int32)],
        compiler_params=pltpu.CompilerParams(vmem_limit_bytes=MIB),
        cost_estimate=pl.CostEstimate(flops=1000000000, bytes_accessed=1000, transcendentals=0),
        name="table",
    )(jnp.stack([dep_owner.T, dep_slot.T]))


def place_item(w, d, x_sc, w_sc, p_sc):
    points, cols = d.shape
    rel = ((d - d[0:1] + cols // 2) & (cols - 1)) - cols // 2
    low = jnp.min(rel, axis=0, keepdims=True)
    base = (d[0:1] + low) & (cols - 1)
    x_sc[...] = (rel - low + (base & (WIN - 1))).astype(jnp.float32)
    w_sc[...] = w.astype(jnp.float32)
    first = lax.broadcasted_iota(jnp.int32, (TILE, LANES), 0)
    places = [(first + i).astype(jnp.float32).astype(jnp.bfloat16) for i in range(0, SPAN, TILE)]
    for t in range(cols // LANES):
        part = slice(t * LANES, (t + 1) * LANES)
        acc = [jnp.zeros((TILE, LANES), jnp.bfloat16)] * len(places)
        for s in range(points):
            x = jnp.broadcast_to(x_sc[s:s + 1, part], (TILE, LANES)).astype(jnp.bfloat16)
            value = jnp.broadcast_to(w_sc[s:s + 1, part], (TILE, LANES)).astype(jnp.bfloat16)
            acc = [jnp.where(place == x, value, total) for place, total in zip(places, acc)]
        for i, total in enumerate(acc):
            p_sc[i * TILE:(i + 1) * TILE, part] = total
    return base // WIN


def place_kernel(slots, table, w_ref, cols_ref, p_ref, q_ref, x_sc, w_sc):
    def one(n, _):
        index = table[0, n]

        @pl.when(index >= 0)
        def _():
            q_ref[n, 0:1, :] = place_item(w_ref[index], cols_ref[index], x_sc, w_sc, p_ref.at[n])

        return 0

    lax.fori_loop(0, slots, one, 0)


def placed(slots, table, weight, places):
    points, cols = weight.shape[1:]
    vmem = pl.BlockSpec(memory_space=pltpu.VMEM)
    return pl.pallas_call(
        functools.partial(place_kernel, slots),
        in_specs=[pl.BlockSpec(memory_space=pltpu.SMEM), vmem, vmem],
        out_specs=[vmem, vmem],
        out_shape=[
            jax.ShapeDtypeStruct((slots, SPAN, cols), jnp.bfloat16),
            jax.ShapeDtypeStruct((slots, 8, cols), jnp.int32),
        ],
        scratch_shapes=[
            pltpu.VMEM((points, cols), jnp.float32),
            pltpu.VMEM((points, cols), jnp.float32),
        ],
        compiler_params=pltpu.CompilerParams(vmem_limit_bytes=8 * MIB),
        cost_estimate=pl.CostEstimate(flops=3000000000, bytes_accessed=1000, transcendentals=0),
        name="place",
    )(table, weight, places)


def item_contribution(v, q, p_ref, v_sc):
    rows, cols = v.shape
    window = jnp.broadcast_to(q.astype(jnp.float32), (rows, cols)).astype(jnp.bfloat16)
    for i in range(cols // WIN):
        v_sc[i * rows:(i + 1) * rows, :] = jnp.where(window == jnp.bfloat16(i), v, jnp.bfloat16(0))
    u = lax.dot_general(
        v_sc[...], p_ref[...], (((1,), (1,)), ((), ())), preferred_element_type=jnp.float32
    )
    u = jnp.concatenate([u, jnp.zeros((u.shape[0], LANES - SPAN), jnp.float32)], 1)
    lane = lax.broadcasted_iota(jnp.int32, (rows, LANES), 1)
    kept, passed = [], []
    for t in range(cols // LANES):
        u0, u1, u2, u3 = (u[(4 * t + j) * rows:(4 * t + j + 1) * rows] for j in range(4))
        kept.append(u0 + pltpu.roll(u1, WIN, 1))
        passed.append(pltpu.roll(u2, 2 * WIN, 1) + pltpu.roll(u3, 3 * WIN, 1))
    return [
        kept[t] + jnp.where(lane >= LANES // 2, passed[t], passed[t - 1]) for t in range(len(kept))
    ]


def stage_kernel(groups, deps, rows, ready, table, v_ref, w_ref, cols_ref, *rest):
    outs, v_sc, places = rest[:len(groups)], rest[len(groups)], rest[len(groups) + 1:]
    cols = v_ref.shape[-1]
    blk = v_ref.shape[0]
    for (firsts, listed), out in zip(groups, outs):
        out[...] = jnp.zeros_like(out)
        for number, first in enumerate(firsts):
            top = number * (2 * CAP * rows + 8)
            if listed:
                ids = lax.broadcasted_iota(jnp.int32, (8, cols), 0)
                slots = jnp.zeros((8, cols), jnp.int32)
                for n in range(2 * CAP):
                    slots = jnp.where(ids == n, table[1, first + n], slots)
                out[top + 2 * CAP * rows:top + 2 * CAP * rows + 8, :] = slots.astype(jnp.float32)

            def one(n, _):
                index = table[0, first + n]

                @pl.when(index >= 0)
                def _():
                    if ready:
                        p, q = w_ref.at[first + n], cols_ref[first + n, 0:1, :]
                    else:
                        x_sc, w_sc, p = places
                        q = place_item(w_ref[index], cols_ref[index], x_sc, w_sc, p)
                    parts = item_contribution(v_ref[lax.div(index, deps)], q, p, v_sc)
                    if listed:
                        at = pl.multiple_of(top + n * rows, 8)
                    else:
                        at = pl.multiple_of((lax.div(n, CAP) * blk + table[1, first + n]) * rows, rows)
                    for t, part in enumerate(parts):
                        where = (pl.ds(at, rows), slice(t * LANES, (t + 1) * LANES))
                        out[where] = out[where] + part

                return 0

            lax.fori_loop(0, 2 * CAP, one, 0)


def stage(groups, deps, ready, table, v, weight, places):
    blk, rows, cols = v.shape
    heights = [len(firsts) * (2 * CAP * rows + 8) if listed else 2 * blk * rows for firsts, listed in groups]
    vmem = pl.BlockSpec(memory_space=pltpu.VMEM)
    return pl.pallas_call(
        functools.partial(stage_kernel, groups, deps, rows, ready),
        in_specs=[pl.BlockSpec(memory_space=pltpu.SMEM), vmem, vmem, vmem],
        out_specs=[vmem] * len(groups),
        out_shape=[jax.ShapeDtypeStruct((height, cols), jnp.float32) for height in heights],
        scratch_shapes=[
            pltpu.VMEM((cols // WIN * rows, cols), jnp.bfloat16),
        ] + ([] if ready else [
            pltpu.VMEM(weight.shape[1:], jnp.float32),
            pltpu.VMEM(weight.shape[1:], jnp.float32),
            pltpu.VMEM((SPAN, cols), jnp.bfloat16),
        ]),
        compiler_params=pltpu.CompilerParams(vmem_limit_bytes=10 * MIB),
        cost_estimate=pl.CostEstimate(
            flops=len(groups) * 200000000, bytes_accessed=500000, transcendentals=0
        ),
        name="stage",
    )(table, v, weight, places)


def merge_kernel(blk, rows, picks, dense_ref, *refs):
    lists, outs = refs[:-2], refs[-2:]
    width = dense_ref.shape[1]
    for half, out in enumerate(outs):
        for c in range(0, width, LANES):
            part = slice(c, c + LANES)
            items = []
            for ref, numbers in zip(lists, picks):
                for top in (number * (2 * CAP * rows + 8) for number in numbers):
                    for n in range(half * CAP, half * CAP + CAP):
                        at, slot = top + n * rows, top + 2 * CAP * rows + n
                        items.append((ref[slot:slot + 1, part], ref[at:at + rows, part]))
            for b in range(blk):
                at = (half * blk + b) * rows
                total = dense_ref[at:at + rows, part]
                for slot, value in items:
                    total = total + jnp.where(slot == float(b), value, 0.0)
                out[b * rows:(b + 1) * rows, part] = total


def merge(blk, rows, dense, *lists):
    width = dense.shape[1]
    return list(pl.pallas_call(
        functools.partial(merge_kernel, blk, rows, [numbers for _, numbers in lists]),
        out_shape=[jax.ShapeDtypeStruct((blk * rows, width), jnp.float32)] * 2,
        compiler_params=pltpu.CompilerParams(vmem_limit_bytes=6 * MIB),
        cost_estimate=pl.CostEstimate(flops=1000000, bytes_accessed=1000000, transcendentals=0),
        name="merge",
    )(dense, *(ref for ref, _ in lists)))


def finish_kernel(blk, rows, sums_ref, here_ref, swapped_ref, out):
    for c in range(0, out.shape[-1], LANES):
        part = slice(c, c + LANES)
        total = sums_ref[:, part] + here_ref[blk * rows:, part] + swapped_ref[:, part]
        out[:, :, part] = jnp.swapaxes(total.reshape(blk, rows, LANES), 0, 1)


def finish(blk, rows, sums, here, swapped):
    return pl.pallas_call(
        functools.partial(finish_kernel, blk, rows),
        out_shape=jax.ShapeDtypeStruct((rows, blk, sums.shape[1]), jnp.float32),
        compiler_params=pltpu.CompilerParams(vmem_limit_bytes=6 * MIB),
        name="finish",
    )(sums, here, swapped)


def edges_kernel(adj0_ref, coef0_ref, adj1_ref, coef1_ref, first_ref, last_ref):
    first_ref[0] = coef0_ref[0] * adj0_ref[0]
    last_ref[0] = coef1_ref[0] * adj1_ref[0]


def edges(adj, coef):
    lev, fields, blk, cols = adj.shape
    shape = (1, fields, blk, cols)
    return pl.pallas_call(
        edges_kernel,
        grid=(1,),
        in_specs=[
            pl.BlockSpec(shape, lambda i: (0, 0, 0, 0)),
            pl.BlockSpec((1, 1, blk, cols), lambda i: (0, 0, 0, 0)),
            pl.BlockSpec(shape, lambda i: (lev - 1, 0, 0, 0)),
            pl.BlockSpec((1, 1, blk, cols), lambda i: (2, lev - 1, 0, 0)),
        ],
        out_specs=[pl.BlockSpec(shape, lambda i: (0, 0, 0, 0))] * 2,
        out_shape=[jax.ShapeDtypeStruct(shape, jnp.float32)] * 2,
        compiler_params=pltpu.CompilerParams(vmem_limit_bytes=60 * MIB),
        name="edges",
    )(adj, coef, adj, coef)


def vertical_kernel(adj_ref, coef_ref, after_ref, before_ref, v_ref):
    lev, fields, blk, cols = adj_ref.shape
    for c in range(0, cols, LANES):
        part = slice(c, c + LANES)
        levels = []
        for m in range(lev):
            low = after_ref[0, :, :, part] if m == lev - 1 else coef_ref[0, m + 1, :, part] * adj_ref[m + 1, :, :, part]
            high = before_ref[0, :, :, part] if m == 0 else coef_ref[2, m - 1, :, part] * adj_ref[m - 1, :, :, part]
            levels.append(low + coef_ref[1, m, :, part] * adj_ref[m, :, :, part] + high)
        whole = jnp.concatenate(levels, 0)
        v_ref[:, :, part] = jnp.swapaxes(whole, 0, 1).astype(jnp.bfloat16)


def vertical(adj, coef, after, before):
    lev, fields, blk, cols = adj.shape
    return pl.pallas_call(
        vertical_kernel,
        out_shape=jax.ShapeDtypeStruct((blk, lev * fields, cols), jnp.bfloat16),
        compiler_params=pltpu.CompilerParams(vmem_limit_bytes=4 * MIB),
        cost_estimate=pl.CostEstimate(flops=1000000, bytes_accessed=1000000, transcendentals=0),
        name="vertical",
    )(adj, coef, after, before)


def shards(adj_arrival, vert_coef, stencil_weight, stencil_cols, dep_owner, dep_slot):
    lev_dev, fields, blk, cols = adj_arrival.shape
    tiles, levels = lax.axis_size("tile"), lax.axis_size("lev")
    deps, points = stencil_weight.shape[1:3]
    items, rows = blk * deps, lev_dev * fields
    chips = tiles // 2
    far = chips // 2

    first, last = edges(adj_arrival, vert_coef)
    after = lax.ppermute(first, "lev", [(i + 1, i) for i in range(levels - 1)])
    before = lax.ppermute(last, "lev", [(i, i + 1) for i in range(levels - 1)])

    table = item_table(chips, dep_owner, dep_slot)
    weight = stencil_weight.reshape(items, points, cols)
    places = stencil_cols.reshape(items, points, cols)
    early = 5 * 2 * CAP
    p, q = placed(early, table, weight, places)
    v = vertical(adj_arrival, vert_coef, after, before)

    sibling = [(t, t ^ 1) for t in range(tiles)]
    ring = [(t, (t + 2 * (1 - 2 * (t % 2))) % tiles) for t in range(tiles)]
    quad = 2 * CAP

    def made(table, *groups):
        ready = max(first for firsts, _ in groups for first in firsts) < early
        return stage(groups, deps, ready, table, v, *((p, q) if ready else (weight, places)))

    def behind(table, value):
        return lax.optimization_barrier((table, value))

    def onward(values, pairs):
        return [lax.ppermute(value, "tile", pairs) for value in values]

    def own_at(h):
        return quad + (far - 1 - h) * 2 * quad

    def other_at(h):
        return own_at(h) + quad

    (listed,) = made(table, ((0,), True))
    table, listed = behind(table, listed)
    (farthest,) = onward([listed], ring)
    near = far - 2
    (others,) = made(table, ((other_at(far - 1), other_at(near)), True))
    table, others = behind(table, others)
    (soon,) = made(table, ((own_at(near),), False))
    table, soon = behind(table, soon)
    (own,) = made(table, ((own_at(far - 1),), True))
    others, farthest, soon = lax.optimization_barrier((others, farthest, soon))
    (given,) = onward([others], sibling)
    table, given = behind(table, given)
    (arrived,) = onward([jnp.concatenate([own, farthest, given[:own.shape[0]]], 0)], ring)

    totals, waiting = None, {near: (given, (1,))}

    def exchanged(table, distances, *others):
        (listed,) = made(table, (tuple(other_at(d) for d in distances), True))
        table, listed, *others = lax.optimization_barrier((table, listed, *others))
        (given,) = onward([listed], sibling)
        waiting.update({d: (given, (number,)) for number, d in enumerate(distances)})
        return table, *others

    for h in range(near, 0, -1):
        (own,) = [soon] if h == near else made(table, ((own_at(h),), False))
        if totals is None:
            table, own = exchanged(table, range(near - 1, 0, -1), own)
            totals = merge(blk, rows, own, waiting[h], (arrived, (0, 1, 2)))
        else:
            mine = lax.optimization_barrier(merge(blk, rows, own, waiting[h]))
            totals = [total + here for total, here in zip(onward(totals, ring), mine)]
        table, totals[0] = behind(table, totals[0])
    sums = onward(totals, ring)
    (here,) = made(table, ((own_at(0),), False))
    (swapped,) = onward([sums[0] + here[:blk * rows]], sibling)
    result = finish(blk, rows, sums[1], here, swapped)
    return result.reshape(lev_dev, fields, blk, cols)


def solution(mesh):
    in_specs = (
        P("lev", None, "tile", None),
        P(None, "lev", "tile", None),
        P("tile", None, None, None),
        P("tile", None, None, None),
        P("tile", None),
        P("tile", None),
    )
    out_specs = P("lev", None, "tile", None)
    return jax.shard_map(shards, mesh=mesh, in_specs=in_specs, out_specs=out_specs, check_vma=False)
```
